512 devices in a mesh: bunch: 64 (over z, x), dom: 8 (over y, core).
Axes of the slice: x: 4, y: 4, z: 16, core: 2. Of those that a mesh axis runs over, the one named last changes fastest.
Arguments:
- positions: float32 [2, 2, 256, 1024], P(None, None, 'bunch', 'dom'), may hold values from -30 to 30
- slice_index: int32 [2, 256, 1024], P(None, 'bunch', 'dom'), may hold values from 0 to 3
- encounters: int32 [256, 7], P('bunch'), may hold values from 0 to 1, as said below
Outputs:
- fields: float32 [2, 256, 4, 2, 64, 64], P(None, 'bunch')
- particle_kicks: float32 [2, 2, 256, 1024], P(None, None, 'bunch', 'dom')
The draws below stay inside these ranges and needn't reach their ends.
Inputs may be any that keep to these rules, and one draw needn't show every extreme that they name: `encounters`: among the 4 rows n * 4 to (n + 1) * 4 - 1 that one index of bunch holds, at most 8 entries are 1 and at least 2; in every draw some such block holds exactly 8. In every such block the first row's column 0 and the last row's column 6 are 1.
All inputs are finite; a program needn't handle non-finite values.
Results may differ from the reference program's by a relative error of at most 0.0003.
Values sent between devices are 32-bit elements; how exact they have to be, the bound alone decides.
A program may use at most 128 MiB of HBM per device.

```python
import jax
import jax.numpy as jnp
import numpy as np
from jax import lax

G = 64
SLICES = 4
R = 3
NOFF = 7
BUN_DEV = 4
NB = 256
NPART = 1024
MAXV = 8


def draw_encounters(key, part):
    key = jax.random.fold_in(key, 7)
    groups = NB // BUN_DEV
    slot_count = BUN_DEV * NOFF
    count_key, top_key, order_key = jax.random.split(key, 3)
    counts = jax.random.randint(count_key, (groups,), MAXV // 4, MAXV + 1)
    fullest = jax.random.randint(top_key, (), 0, groups)
    counts = jnp.where(jnp.arange(groups) == fullest, MAXV, counts)
    scores = jax.random.randint(order_key, (groups, slot_count), 0, 1 << 20) * slot_count
    scores = scores + jnp.arange(slot_count, dtype=jnp.int32)[None, :]
    slot_ids = jnp.arange(slot_count, dtype=jnp.int32)[None, :]
    scores = jnp.where(slot_ids == 0, -2, scores)
    scores = jnp.where(slot_ids == slot_count - 1, -1, scores)
    ordering = jnp.argsort(scores, axis=1)
    slot_rank = jnp.argsort(ordering, axis=1)
    live_slots = (slot_rank < counts[:, None]).astype(jnp.int32)
    return live_slots.reshape(NB, NOFF)


def set_ends(values, rng, smallest, top_value):
    spot = [jax.random.randint(jax.random.fold_in(rng, axis), (), 0, length) for axis, length in enumerate(values.shape)]
    widest = values.shape.index(max(values.shape))
    neighbour = spot[:widest] + [(spot[widest] + 1) % values.shape[widest]] + spot[widest + 1:]
    return values.at[tuple(spot)].set(smallest).at[tuple(neighbour)].set(top_value)


def block_scale(key, extent, shards, smallest, largest):
    def one(position, parts):
        draws = jax.random.uniform(jax.random.fold_in(jax.random.fold_in(key, 6), position), (parts,), jnp.float32, smallest / len(shards), largest / len(shards))
        return jnp.repeat(jnp.exp(draws), extent[position] // parts).reshape((-1,) + (1,) * (len(extent) - position - 1))

    gain = one(*shards[0])
    for cut in shards[1:]:
        gain = gain * one(*cut)
    return gain


def normal_values(stream_key, shape, scale, most, cuts=(), kind=jnp.bfloat16):
    entries = scale * jax.random.normal(stream_key, shape, jnp.float32)
    if cuts:
        entries = entries * block_scale(stream_key, shape, cuts, -0.22, 0.18)
    return jnp.clip(entries, -most, most).astype(kind)


def setup_inputs(seed: int = 0) -> dict:
    splits = jax.random.split(jax.random.key(seed), 4)
    positions = normal_values(splits[0], (2, 2, NB, NPART), (G / 8), 30.0, ((2, 64), (3, 8)), jnp.float32)
    slice_index = set_ends(jax.random.randint(splits[1], (2, NB, NPART), 0, SLICES), jax.random.fold_in(splits[1], 1), 0, SLICES - 1).astype(jnp.int32)
    encounters = draw_encounters(jax.random.fold_in(splits[3], 71), 0)
    return dict(positions=positions, slice_index=slice_index, encounters=encounters)


CHARGE = 8.0
SOFTEN = 1.0
HIGHEST = lax.Precision.HIGHEST


def tent_weights(coordinate, cell_count):
    centre = 0.5 * (cell_count - 1)
    grid_points = jnp.arange(cell_count, dtype=jnp.float32)
    offset = centre + coordinate[..., None, :] - grid_points[:, None]
    return jnp.maximum(0.0, 1.0 - jnp.abs(offset))


def kernel_space(column, cells_pad, slices, half_range):
    half_cells = cells_pad // 2
    cell_index = jnp.arange(cells_pad, dtype=jnp.int32)
    signed = jnp.where(cell_index < half_cells, cell_index, cell_index - cells_pad).astype(jnp.float32)
    slice_gap = jnp.arange(2 * slices - 1, dtype=jnp.int32) - (slices - 1)
    column_lead = jnp.asarray(column, jnp.int32) - half_range
    shift_x = (20 * column_lead[..., None] + 4 * slice_gap).astype(jnp.float32)
    shift_y = (3 * column_lead[..., None] + slice_gap).astype(jnp.float32)
    along_x = signed[:, None] + shift_x[..., None, None]
    along_y = signed[None, :] + shift_y[..., None, None]
    spread = along_x * along_x + along_y * along_y + SOFTEN
    return jnp.stack([along_x / spread, along_y / spread], axis=-3)


def reference(positions, slice_index, encounters):
    flat_x = positions[0].reshape(2 * NB, NPART)
    flat_y = positions[1].reshape(2 * NB, NPART)
    flat_slice = slice_index.reshape(2 * NB, NPART)
    slice_ids = jnp.arange(SLICES, dtype=jnp.int32)

    def deposit(bundle):
        coord_x, coord_y, labels = bundle
        weight_x = tent_weights(coord_x, G)
        weight_y = tent_weights(coord_y, G)
        slice_mask = (labels[None, :] == slice_ids[:, None]).astype(jnp.float32)
        masked_y = slice_mask[:, None, :] * weight_y[None]
        return jnp.einsum("ip,sjp->sij", weight_x, masked_y, precision=HIGHEST) * (CHARGE / NPART)

    charge = lax.map(deposit, (flat_x, flat_y, flat_slice)).reshape(2, NB, SLICES, G, G)
    kernels = kernel_space(jnp.arange(NOFF, dtype=jnp.int32), 2 * G, SLICES, R)
    kernel_hats = jnp.fft.fft2(kernels)
    gap_table = np.arange(SLICES)[:, None] - np.arange(SLICES)[None, :] + SLICES - 1

    def transform_charge(grid_values):
        return jnp.fft.fft2(jnp.pad(grid_values, ((0, 0), (0, G), (0, G))))

    near_fields = jnp.zeros((NB, SLICES, 2, G, G), jnp.float32)
    far_fields = jnp.zeros((NB, SLICES, 2, G, G), jnp.float32)
    bunch_ids = jnp.arange(NB, dtype=jnp.int32)
    for column in range(NOFF):
        paired = kernel_hats[column][gap_table]

        def one_pair(bunch_id):
            partner = (bunch_id + column - R) % NB
            first_hat = transform_charge(charge[0, bunch_id])
            second = transform_charge(charge[1, partner])
            on_first = jnp.sum(paired * second[None, :, None], axis=1)
            on_second = jnp.sum(-jnp.conj(paired) * first_hat[:, None, None], axis=0)
            live_flag = encounters[bunch_id, column].astype(jnp.float32)
            first_field = jnp.real(jnp.fft.ifft2(on_first))[..., :G, :G]
            second_field = jnp.real(jnp.fft.ifft2(on_second))[..., :G, :G]
            return live_flag * first_field, live_flag * second_field

        on_first, on_second = lax.map(one_pair, bunch_ids)
        near_fields = near_fields + on_first
        far_fields = far_fields + jnp.roll(on_second, column - R, axis=0)

    fields = jnp.stack([near_fields, far_fields])
    flat_fields = fields.reshape(2 * NB, SLICES, 2, G, G)

    def kick(bundle):
        grid_fields, coord_x, coord_y, labels = bundle
        weight_x = tent_weights(coord_x, G)
        weight_y = tent_weights(coord_y, G)
        slice_mask = (labels[None, :] == slice_ids[:, None]).astype(jnp.float32)
        sampled = jnp.einsum("scij,jp->scip", grid_fields, weight_y, precision=HIGHEST)
        values = jnp.einsum("ip,scip->scp", weight_x, sampled, precision=HIGHEST)
        return jnp.sum(slice_mask[:, None, :] * values, axis=0)

    particle_kicks = lax.map(kick, (flat_fields, flat_x, flat_y, flat_slice))
    particle_kicks = jnp.transpose(particle_kicks.reshape(2, NB, 2, NPART), (2, 0, 1, 3))
    return fields, particle_kicks
```

```python
import functools

import jax
import jax.numpy as jnp
import ml_dtypes
import numpy as np
from jax import lax
from jax.experimental import pallas as pl
from jax.experimental.pallas import tpu as pltpu
from jax.sharding import PartitionSpec as P

G = 64
SLICES = 4
R = 3
NOFF = 7
CHARGE = 8.0
SOFTEN = 1.0

BUN = 4
SRC = BUN + 2 * R
N1 = 152
N2 = 134
ROWS = 80
MESH = pl.DeviceIdType.MESH
BF = jnp.bfloat16
F32 = jnp.float32


def split_table(values):
    high = values.astype(ml_dtypes.bfloat16)
    low = (values - high.astype(np.float64)).astype(ml_dtypes.bfloat16)
    return high, low


@functools.lru_cache(maxsize=None)
def tables(scale):
    line = np.arange(ROWS)
    kx = np.arange(ROWS)
    live_kx = (kx <= N1 // 2).astype(np.float64)
    ky = np.arange(128)
    live_ky = (ky <= N2 // 2).astype(np.float64)

    phase_y = 2.0 * np.pi * (line[:, None] * ky[None, :] % N2) / N2
    along = np.concatenate([np.cos(phase_y) * live_ky, -np.sin(phase_y) * live_ky], axis=1)
    fwd_y = split_table(np.concatenate([along, along], axis=0))

    phase_x = 2.0 * np.pi * (kx[:, None] * line[None, :] % N1) / N1
    cos_x = np.cos(phase_x) * live_kx[:, None]
    sin_x = np.sin(phase_x) * live_kx[:, None]
    high, low = split_table(np.concatenate([cos_x, sin_x], axis=0))
    fwd_x = np.concatenate([high, high, low], axis=1)

    half = np.where((kx == 0) | (kx == N1 // 2), 0.5, 1.0) / (N1 * N2)
    high, low = split_table(np.concatenate([(cos_x * half[:, None]).T, (sin_x * half[:, None]).T], axis=1))
    inv_x = np.concatenate([high, low], axis=0)

    twice = np.where((ky == 0) | (ky == N2 // 2), 1.0, 2.0) * live_ky
    cell = np.arange(128)
    live_cell = (cell < G + SLICES - 1).astype(np.float64)
    phase = 2.0 * np.pi * (ky[:, None] * cell[None, :] % N2) / N2
    back = np.concatenate([np.cos(phase) * twice[:, None], -np.sin(phase) * twice[:, None]], axis=0)
    inv_y = np.concatenate(split_table(back * live_cell[None, :]), axis=1)

    d1 = np.arange(N1)
    d1 = np.where(d1 < N1 // 2, d1, d1 - N1).astype(np.float64)
    d2 = np.arange(N2)
    d2 = np.where(d2 < N2 // 2, d2, d2 - N2).astype(np.float64)
    spectra = np.zeros((NOFF, 2, 2, 2 * ROWS, 128), np.float32)
    rows = np.arange(N1 // 2 + 1)
    for column in range(NOFF):
        along_x = d1[:, None] + 20.0 * (column - R)
        along_y = d2[None, :] + 3.0 * (column - R)
        spread = along_x * along_x + along_y * along_y + SOFTEN
        for part, value in enumerate((along_x / spread, along_y / spread)):
            hat = np.fft.fft2(value)[:, : N2 // 2 + 1] * scale
            for half_index, pick in enumerate((rows, (-rows) % N1)):
                place = slice(half_index * ROWS, half_index * ROWS + rows.size)
                spectra[column, part, 0, place, : N2 // 2 + 1] = hat[pick].real
                spectra[column, part, 1, place, : N2 // 2 + 1] = hat[pick].imag
    return fwd_y + (fwd_x, inv_x, inv_y, spectra)


def exchange_kernel(
    groups, doms,
    pos_any, sl_any, enc_any, g_ref, e_ref,
    pos_ref, sl_ref, enc_ref, block, encs, in_sem, send_sem, esend_sem, recv_sem, erecv_sem,
):
    n = lax.axis_index("bunch")
    me = lax.axis_index("dom")
    loads = [
        pltpu.make_async_copy(src, dst, in_sem.at[k])
        for k, (src, dst) in enumerate(((pos_any, pos_ref), (sl_any, sl_ref), (enc_any, enc_ref)))
    ]
    for load in loads:
        load.start()
    peers = []
    for off in (0, 1, -1):
        for j in range(doms):
            if off == 0 and j == 0:
                continue
            peers.append((off, lax.rem(n + off + groups, groups), lax.rem(me + j, doms)))

    barrier = pltpu.get_barrier_semaphore()
    for _, there, dom in peers:
        pl.semaphore_signal(barrier, inc=1, device_id=(there, dom), device_id_type=MESH)

    for load in loads:
        load.wait()
    centre = 0.5 * (G - 1)
    for beam in range(2):
        gap = sl_ref[beam].astype(F32)
        block[beam * 8 : beam * 8 + 4, :] = (centre + pos_ref[0, beam]) + 4.0 * gap
        block[beam * 8 + 4 : beam * 8 + 8, :] = (centre + pos_ref[1, beam]) + gap
    encs[...] = jnp.zeros_like(encs)
    encs[0:BUN, 0:NOFF] = enc_ref[...]
    pl.semaphore_wait(barrier, len(peers))

    sends = []
    for k, off in enumerate((1, -1)):
        copy = pltpu.make_async_remote_copy(
            src_ref=encs,
            dst_ref=e_ref.at[1 - off],
            send_sem=esend_sem.at[k],
            recv_sem=erecv_sem.at[1 - off],
            device_id=(lax.rem(n + off + groups, groups), me),
            device_id_type=MESH,
        )
        copy.start()
        sends.append(copy)
    for k, (off, there, dom) in enumerate(peers):
        copy = pltpu.make_async_remote_copy(
            src_ref=block,
            dst_ref=g_ref.at[1 - off, me],
            send_sem=send_sem.at[k],
            recv_sem=recv_sem.at[1 - off, me],
            device_id=(there, dom),
            device_id_type=MESH,
        )
        copy.start()
        sends.append(copy)
    mine = pltpu.make_async_copy(block, g_ref.at[1, me], recv_sem.at[1, me])
    mine.start()
    mine_e = pltpu.make_async_copy(encs, e_ref.at[1], erecv_sem.at[1])
    mine_e.start()
    for grp in range(3):
        for d in range(doms):
            pltpu.make_async_copy(block, g_ref.at[grp, d], recv_sem.at[grp, d]).wait()
        pltpu.make_async_copy(encs, e_ref.at[grp], erecv_sem.at[grp]).wait()
    for copy in sends:
        copy.wait_send()


def high_low(values):
    high = values.astype(BF)
    return high, (values - high.astype(F32)).astype(BF)


def mm(a, b):
    return jnp.dot(a, b, preferred_element_type=F32)


def live_lists(enc_ref, order, place, pair_c, pair_p, pair_count):
    flags = []
    for beam in range(2):
        for b in range(BUN):
            row = []
            for c in range(NOFF):
                if beam == 0:
                    row.append(enc_ref[1, b, c])
                else:
                    a = b + c + 1
                    row.append(enc_ref[a // BUN, a % BUN, 2 * R - c])
            flags.append(row)
    count = jnp.int32(0)
    for k in range(2 * SRC + 8):
        order[k] = 0
    for source in range(2 * SRC):
        beam, m = source // SRC, source % SRC
        users = [flags[(1 - beam) * BUN + b][m - b] for b in range(BUN) if 0 <= m - b < NOFF]
        need = users[0]
        for other in users[1:]:
            need = jnp.maximum(need, other)
        order[count] = source
        place[source] = count
        count = count + need
    order[count] = 0
    for target in range(2 * BUN):
        beam, b = target // BUN, target % BUN
        total = jnp.int32(0)
        for c in range(NOFF):
            pair_c[target * 8 + total] = c
            pair_p[target * 8 + total] = place[(1 - beam) * SRC + b + c]
            total = total + flags[target][c]
        pair_count[target] = total
    return count


def solve_kernel(
    doms,
    g_ref, enc_ref, fyh_any, fyl_any, fx_any, ix_any, iy_any, kv_any,
    f_any, kick_ref,
    fyh_ref, fyl_ref, fx_ref, ix_ref, iy_ref, kv, table_sem,
    wx, wy, grids, spec, acc, bh_ref, bl_ref, win,
    order, place, pair_c, pair_p, pair_count, out_sem,
):
    pairs = (
        (fyh_any, fyh_ref), (fyl_any, fyl_ref), (fx_any, fx_ref),
        (kv_any, kv), (ix_any, ix_ref), (iy_any, iy_ref),
    )
    loads = [pltpu.make_async_copy(src, dst, table_sem.at[k]) for k, (src, dst) in enumerate(pairs)]
    for load in loads:
        load.start()

    count = live_lists(enc_ref, order, place, pair_c, pair_p, pair_count)
    line = lax.broadcasted_iota(jnp.int32, (16, 128), 0).astype(F32)
    lines = [line + 16.0 * t for t in range(ROWS // 16)]

    def weights(k, dest_x, dest_y):
        source = order[k]
        beam = source // SRC
        m = source - beam * SRC
        grp = (m + 1) // BUN
        bunch = (m + 1) % BUN
        for coord, dest in ((0, dest_x), (1, dest_y)):
            row = beam * 8 + coord * 4 + bunch
            for d in range(doms):
                at = jnp.broadcast_to(g_ref[grp, d, pl.ds(row, 1), :], (16, 128))
                cols = slice(d * 128, (d + 1) * 128)
                for t in range(ROWS // 16):
                    high, low = high_low(jnp.maximum(0.0, 1.0 - jnp.abs(at - lines[t])))
                    dest[16 * t : 16 * t + 16, cols] = high
                    dest[ROWS + 16 * t : ROWS + 16 * t + 16, cols] = low

    def deposit(src_x, src_y, grid):
        both = lax.dot_general(src_x[...], src_y[...], (((1,), (1,)), ((), ())), preferred_element_type=F32)
        ah, al = high_low(both[:ROWS] + both[ROWS:])
        grid[0] = ah
        grid[1] = al

    def spectra(k, grids):
        ah = [grid[0] for grid in grids]
        al = [grid[1] for grid in grids]
        rows = len(grids) * ROWS
        first = mm(jnp.concatenate(ah + al, axis=0), fyh_ref[...])
        first = first[:rows] + first[rows:] + mm(jnp.concatenate(ah, axis=0), fyl_ref[...])
        for s in range(len(grids)):
            rh, rl = high_low(first[s * ROWS : (s + 1) * ROWS])
            out = mm(fx_ref[...], jnp.concatenate([rh, rl, rh], axis=0))
            cr, ci = out[:ROWS, :128], out[:ROWS, 128:]
            sr, si = out[ROWS:, :128], out[ROWS:, 128:]
            spec[k + s, 0, :ROWS] = cr + si
            spec[k + s, 0, ROWS:] = cr - si
            spec[k + s, 1, :ROWS] = ci - sr
            spec[k + s, 1, ROWS:] = ci + sr

    weights(0, wx[0], wy[0])
    weights(1, wx[1], wy[1])
    for load in loads[:3]:
        load.wait()

    def four_sources(j, _):
        k = 4 * j
        spectra(k, grids[2:])
        for s in range(2):
            deposit(wx[s], wy[s], grids[s])
            weights(k + 2 + s, wx[2 + s], wy[2 + s])
        spectra(k + 2, grids[:2])
        for s in range(2):
            deposit(wx[2 + s], wy[2 + s], grids[2 + s])
            weights(k + 4 + s, wx[s], wy[s])
        return 0

    turns = (count + 3) // 4
    lax.fori_loop(0, turns, four_sources, 0)
    spectra(4 * turns, grids[2:])
    for load in loads[3:]:
        load.wait()

    me = lax.axis_index("dom")
    index = lax.broadcasted_iota(jnp.int32, (ROWS, 128), 0).astype(F32)

    def multiply(target, _):
        acc[target] = jnp.zeros_like(acc[target])

        def partner(j, _):
            c = pair_c[target * 8 + j]
            p = pair_p[target * 8 + j] + 2
            for t in range(2 * ROWS // 16):
                rows = slice(16 * t, 16 * t + 16)
                re = spec[p, 0, rows]
                im = spec[p, 1, rows]
                for part in range(2):
                    kr = kv[c, part, 0, rows]
                    ki = kv[c, part, 1, rows]
                    acc[target, part, 0, rows] += kr * re - ki * im
                    acc[target, part, 1, rows] += kr * im + ki * re
            return 0

        lax.fori_loop(0, pair_count[target], partner, 0)
        return 0

    lax.fori_loop(0, 2 * BUN, multiply, 0)

    def finish(beam, _):
        for b in range(BUN):
            target = beam * BUN + b
            for part in range(2):
                rp, rm = acc[target, part, 0, :ROWS], acc[target, part, 0, ROWS:]
                ip, im = acc[target, part, 1, :ROWS], acc[target, part, 1, ROWS:]
                top = jnp.concatenate([rp + rm, ip + im], axis=1)
                low = jnp.concatenate([im - ip, rp - rm], axis=1)
                dh, dl = high_low(jnp.concatenate([top, low], axis=0))
                first = mm(ix_ref[...], dh)
                bh, bl = high_low(first[:ROWS] + first[ROWS:] + mm(ix_ref[:ROWS], dl))
                bh_ref[b, part * ROWS : (part + 1) * ROWS] = bh
                bl_ref[b, part * ROWS : (part + 1) * ROWS] = bl
        for b in range(BUN):
            wide = mm(bh_ref[b], iy_ref[...])
            field = wide[:, :128] + wide[:, 128:] + mm(bl_ref[b], iy_ref[:, :128])
            for part in range(2):
                for i in range(SLICES):
                    win[beam, b, i, part] = field[part * ROWS + 4 * i : part * ROWS + 4 * i + G, i : i + G]

            x = jnp.broadcast_to(g_ref[1, me, pl.ds(beam * 8 + b, 1), :], (ROWS, 128))
            y = jnp.broadcast_to(g_ref[1, me, pl.ds(beam * 8 + 4 + b, 1), :], (ROWS, 128))
            weight_x = jnp.maximum(0.0, 1.0 - jnp.abs(x - index))
            yh, yl = high_low(jnp.maximum(0.0, 1.0 - jnp.abs(y - index)))
            fh, fl = high_low(field[:, :ROWS])
            first = mm(jnp.concatenate([fh, fl], axis=0), jnp.concatenate([yh, yl], axis=1))
            sampled = first[: 2 * ROWS, :128] + first[2 * ROWS :, :128] + first[: 2 * ROWS, 128:]
            for part in range(2):
                kick_ref[part, beam, b : b + 1, :] = jnp.sum(
                    weight_x * sampled[part * ROWS : (part + 1) * ROWS], axis=0, keepdims=True
                )
        pltpu.make_async_copy(win.at[beam], f_any.at[beam], out_sem.at[beam]).start()
        return 0

    lax.fori_loop(0, 2, finish, 0)
    for beam in range(2):
        pltpu.make_async_copy(win.at[beam], f_any.at[beam], out_sem.at[beam]).wait()


def solve(gathered, enc):
    doms, particles = gathered.shape[1], gathered.shape[3]
    vmem = pl.BlockSpec(memory_space=pltpu.VMEM)
    anywhere = pl.BlockSpec(memory_space=pl.ANY)
    consts = [jnp.asarray(t) for t in tables(CHARGE / (particles * doms))]
    weight = pltpu.VMEM((2 * ROWS, doms * particles), BF)
    return pl.pallas_call(
        functools.partial(solve_kernel, doms),
        out_shape=(
            jax.ShapeDtypeStruct((2, BUN, SLICES, 2, G, G), F32),
            jax.ShapeDtypeStruct((2, 2, BUN, particles), F32),
        ),
        in_specs=[vmem, pl.BlockSpec(memory_space=pltpu.SMEM)] + [anywhere] * 6,
        out_specs=(anywhere, vmem),
        scratch_shapes=[pltpu.VMEM(t.shape, t.dtype) for t in consts] + [
            pltpu.SemaphoreType.DMA((len(consts),)),
            [weight] * 4,
            [weight] * 4,
            [pltpu.VMEM((2, ROWS, 2 * ROWS), BF)] * 4,
            pltpu.VMEM((2 * SRC + 4, 2, 2 * ROWS, 128), F32),
            pltpu.VMEM((2 * BUN, 2, 2, 2 * ROWS, 128), F32),
            pltpu.VMEM((BUN, 2 * ROWS, 256), BF),
            pltpu.VMEM((BUN, 2 * ROWS, 256), BF),
            pltpu.VMEM((2, BUN, SLICES, 2, G, G), F32),
            pltpu.SMEM((2 * SRC + 8,), jnp.int32),
            pltpu.SMEM((2 * SRC,), jnp.int32),
            pltpu.SMEM((2 * BUN * 8,), jnp.int32),
            pltpu.SMEM((2 * BUN * 8,), jnp.int32),
            pltpu.SMEM((2 * BUN,), jnp.int32),
            pltpu.SemaphoreType.DMA((2,)),
        ],
        compiler_params=pltpu.CompilerParams(vmem_limit_bytes=24 * 1024 * 1024),
        name="solve",
    )(gathered, enc, *[pltpu.with_memory_space_constraint(t, pltpu.HBM) for t in consts])


def on_device(positions, slice_index, encounters):
    groups, doms = lax.axis_size("bunch"), lax.axis_size("dom")
    particles = positions.shape[3]
    anywhere = pl.BlockSpec(memory_space=pl.ANY)
    gathered, enc = pl.pallas_call(
        functools.partial(exchange_kernel, groups, doms),
        out_shape=(
            jax.ShapeDtypeStruct((3, doms, 16, particles), F32),
            jax.ShapeDtypeStruct((3, 8, 128), jnp.int32),
        ),
        in_specs=[anywhere] * 3,
        out_specs=(anywhere, anywhere),
        scratch_shapes=[
            pltpu.VMEM(positions.shape, F32),
            pltpu.VMEM(slice_index.shape, jnp.int32),
            pltpu.VMEM(encounters.shape, jnp.int32),
            pltpu.VMEM((16, particles), F32),
            pltpu.VMEM((8, 128), jnp.int32),
            pltpu.SemaphoreType.DMA((3,)),
            pltpu.SemaphoreType.DMA((3 * doms - 1,)),
            pltpu.SemaphoreType.DMA((2,)),
            pltpu.SemaphoreType.DMA((3, doms)),
            pltpu.SemaphoreType.DMA((3,)),
        ],
        compiler_params=pltpu.CompilerParams(
            collective_id=0, has_side_effects=True, vmem_limit_bytes=1024 * 1024
        ),
        name="exchange",
    )(*[pltpu.with_memory_space_constraint(v, pltpu.HBM) for v in (positions, slice_index, encounters)])
    return solve(gathered, enc)


def solution(mesh):
    placed = (P(None, None, "bunch", "dom"), P(None, "bunch", "dom"), P("bunch", None))
    return jax.shard_map(
        on_device,
        mesh=mesh,
        in_specs=placed,
        out_specs=(P(None, "bunch", None, None, None, None), P(None, None, "bunch", "dom")),
        check_vma=False,
    )
```

```python
import functools

import jax
import jax.numpy as jnp
import ml_dtypes
import numpy as np
from jax import lax
from jax.experimental import pallas as pl
from jax.experimental.pallas import tpu as pltpu
from jax.sharding import PartitionSpec as P

G = 64
SLICES = 4
R = 3
NOFF = 7
CHARGE = 8.0
SOFTEN = 1.0

BUN = 4
SRC = BUN + 2 * R
ALWAYS = (SRC, 2 * SRC - 1, R - 1, R + BUN)
N1 = 152
N2 = 134
ROWS = 80
MESH = pl.DeviceIdType.MESH
BF = jnp.bfloat16
F32 = jnp.float32


def split_table(values):
    high = values.astype(ml_dtypes.bfloat16)
    low = (values - high.astype(np.float64)).astype(ml_dtypes.bfloat16)
    return high, low


@functools.lru_cache(maxsize=None)
def tables(scale):
    line = np.arange(ROWS)
    kx = np.arange(ROWS)
    live_kx = (kx <= N1 // 2).astype(np.float64)
    ky = np.arange(128)
    live_ky = (ky <= N2 // 2).astype(np.float64)

    phase_y = 2.0 * np.pi * (line[:, None] * ky[None, :] % N2) / N2
    along = np.concatenate([np.cos(phase_y) * live_ky, -np.sin(phase_y) * live_ky], axis=1)
    high, low = split_table(along)
    fwd_y = np.concatenate([np.concatenate([high, high], axis=0), np.concatenate([low, low], axis=0)], axis=1)

    phase_x = 2.0 * np.pi * (kx[:, None] * line[None, :] % N1) / N1
    cos_x = np.cos(phase_x) * live_kx[:, None]
    sin_x = np.sin(phase_x) * live_kx[:, None]
    high, low = split_table(np.concatenate([cos_x, sin_x], axis=0))
    fwd_x = np.concatenate([high, high, low], axis=1)

    half = np.where((kx == 0) | (kx == N1 // 2), 0.5, 1.0) / (N1 * N2)
    high, low = split_table(np.concatenate([(cos_x * half[:, None]).T, (sin_x * half[:, None]).T], axis=1))
    inv_x = np.concatenate([high, high, low], axis=1)

    twice = np.where((ky == 0) | (ky == N2 // 2), 1.0, 2.0) * live_ky
    cell = np.arange(128)
    live_cell = (cell < G + SLICES - 1).astype(np.float64)
    phase = 2.0 * np.pi * (ky[:, None] * cell[None, :] % N2) / N2
    back = np.concatenate([np.cos(phase) * twice[:, None], -np.sin(phase) * twice[:, None]], axis=0)
    inv_y = np.concatenate(split_table(back * live_cell[None, :]), axis=1)

    d1 = np.arange(N1)
    d1 = np.where(d1 < N1 // 2, d1, d1 - N1).astype(np.float64)
    d2 = np.arange(N2)
    d2 = np.where(d2 < N2 // 2, d2, d2 - N2).astype(np.float64)
    spectra = np.zeros((NOFF, 2, 2, 2 * ROWS, 128), np.float32)
    rows = np.arange(N1 // 2 + 1)
    for column in range(NOFF):
        along_x = d1[:, None] + 20.0 * (column - R)
        along_y = d2[None, :] + 3.0 * (column - R)
        spread = along_x * along_x + along_y * along_y + SOFTEN
        for part, value in enumerate((along_x / spread, along_y / spread)):
            hat = np.fft.fft2(value)[:, : N2 // 2 + 1] * scale
            for half_index, pick in enumerate((rows, (-rows) % N1)):
                place = slice(half_index * ROWS, half_index * ROWS + rows.size)
                spectra[column, part, 0, place, : N2 // 2 + 1] = hat[pick].real
                spectra[column, part, 1, place, : N2 // 2 + 1] = hat[pick].imag
    return fwd_y, fwd_x, inv_x, inv_y, spectra


def exchange_kernel(
    groups, doms,
    pos_any, sl_any, enc_any, g_ref, e_ref,
    pos_ref, sl_ref, enc_ref, block, encs, in_sem, sems,
):
    n = lax.axis_index("bunch")
    me = lax.axis_index("dom")
    loads = [
        pltpu.make_async_copy(src, dst, in_sem.at[k])
        for k, (src, dst) in enumerate(((pos_any, pos_ref), (sl_any, sl_ref), (enc_any, enc_ref)))
    ]
    for load in loads:
        load.start()
    peers = []
    for off in (1, -1, 0):
        for j in range(doms):
            if off == 0 and j == 0:
                continue
            peers.append((off, lax.rem(n + off + groups, groups), lax.rem(me + j, doms)))

    barrier = pltpu.get_barrier_semaphore()
    for _, there, dom in peers:
        pl.semaphore_signal(barrier, inc=1, device_id=(there, dom), device_id_type=MESH)

    for load in loads:
        load.wait()
    centre = 0.5 * (G - 1)
    for beam in range(2):
        gap = sl_ref[beam].astype(F32)
        block[beam * 8 : beam * 8 + 4, :] = (centre + pos_ref[0, beam]) + 4.0 * gap
        block[beam * 8 + 4 : beam * 8 + 8, :] = (centre + pos_ref[1, beam]) + gap
    encs[...] = jnp.zeros_like(encs)
    encs[0:BUN, 0:NOFF] = enc_ref[...]
    pl.semaphore_wait(barrier, len(peers))

    for off in (1, -1):
        pltpu.make_async_remote_copy(
            src_ref=encs,
            dst_ref=e_ref.at[1 - off],
            send_sem=sems.at[0],
            recv_sem=sems.at[1],
            device_id=(lax.rem(n + off + groups, groups), me),
            device_id_type=MESH,
        ).start()
    for off, there, dom in peers:
        pltpu.make_async_remote_copy(
            src_ref=block,
            dst_ref=g_ref.at[(1 - off) * doms + me],
            send_sem=sems.at[2],
            recv_sem=sems.at[3],
            device_id=(there, dom),
            device_id_type=MESH,
        ).start()
    pltpu.make_async_copy(encs, e_ref.at[1], sems.at[1]).start()
    pltpu.make_async_copy(block, g_ref.at[doms + me], sems.at[3]).start()
    for sem, ref in ((3, g_ref), (1, e_ref), (2, g_ref.at[pl.ds(0, len(peers))]), (0, e_ref.at[pl.ds(0, 2)])):
        pltpu.make_async_copy(ref, ref, sems.at[sem]).wait()


def high_low(values):
    high = values.astype(BF)
    return high, (values - high.astype(F32)).astype(BF)


def mm(a, b):
    return jnp.dot(a, b, preferred_element_type=F32)


def live_lists(enc_ref, order, place, pair_c, pair_p, pair_count):
    flags = []
    for beam in range(2):
        for b in range(BUN):
            row = []
            for c in range(NOFF):
                if beam == 0:
                    row.append(enc_ref[1, b, c])
                else:
                    a = b + c + 1
                    row.append(enc_ref[a // BUN, a % BUN, 2 * R - c])
            flags.append(row)
    count = jnp.int32(0)
    for k in range(2 * SRC + 8):
        order[k] = 0
    for source in ALWAYS:
        place[source] = count
        order[count] = source
        count = count + 1
    for source in range(2 * SRC):
        if source in ALWAYS:
            continue
        beam, m = source // SRC, source % SRC
        users = [flags[(1 - beam) * BUN + b][m - b] for b in range(BUN) if 0 <= m - b < NOFF]
        need = users[0]
        for other in users[1:]:
            need = jnp.maximum(need, other)
        order[count] = source
        place[source] = count
        count = count + need
    order[count] = 0
    for target in range(2 * BUN):
        beam, b = target // BUN, target % BUN
        total = jnp.int32(0)
        for c in range(NOFF):
            pair_c[target * 8 + total] = c
            pair_p[target * 8 + total] = place[(1 - beam) * SRC + b + c]
            total = total + flags[target][c]
        pair_count[target] = total
    return count


def solve_kernel(
    doms,
    g_ref, enc_any, fy_any, fx_any, ix_any, iy_any, kv_any,
    f_any, kick_any,
    fy_ref, fx_ref, ix_ref, iy_ref, kv, table_sem,
    wx, wy, grids, spec, acc, bh_ref, bl_ref, win, kick_ref,
    enc_ref, order, place, pair_c, pair_p, pair_count, enc_sem, out_sem,
):
    enc_load = pltpu.make_async_copy(enc_any, enc_ref, enc_sem)
    enc_load.start()
    pairs = ((fy_any, fy_ref), (fx_any, fx_ref), (kv_any, kv), (ix_any, ix_ref), (iy_any, iy_ref))
    loads = [pltpu.make_async_copy(src, dst, table_sem.at[k]) for k, (src, dst) in enumerate(pairs)]
    for load in loads:
        load.start()

    line = lax.broadcasted_iota(jnp.int32, (16, 128), 0).astype(F32)
    lines = [line + 16.0 * t for t in range(ROWS // 16)]

    def weights(source, slot):
        beam = source // SRC
        m = source - beam * SRC
        grp = (m + 1) // BUN
        bunch = (m + 1) % BUN
        for coord, dest in ((0, wx[slot]), (1, wy[slot])):
            row = beam * 8 + coord * 4 + bunch
            for d in range(doms):
                at = jnp.broadcast_to(g_ref[grp * doms + d, pl.ds(row, 1), :], (16, 128))
                cols = slice(d * 128, (d + 1) * 128)
                for t in range(ROWS // 16):
                    high, low = high_low(jnp.maximum(0.0, 1.0 - jnp.abs(at - lines[t])))
                    dest[16 * t : 16 * t + 16, cols] = high
                    dest[ROWS + 16 * t : ROWS + 16 * t + 16, cols] = low

    def deposit(slot):
        both = lax.dot_general(
            wx[slot][...], wy[slot][...], (((1,), (1,)), ((), ())), preferred_element_type=F32
        )
        high, low = high_low(both[:ROWS] + both[ROWS:])
        grids[slot][:ROWS] = high
        grids[slot][ROWS:] = low

    def spectra(k, slots):
        grid = [grids[slot][:ROWS] for slot in slots]
        wide = len(slots) * ROWS
        low = [grids[slot][ROWS:] for slot in slots]
        first = mm(jnp.concatenate(grid + low, axis=0), fy_ref[:, :256])
        first = first[:wide] + first[wide:] + mm(jnp.concatenate(grid, axis=0), fy_ref[:, 256:])
        for s in range(len(slots)):
            high, low = high_low(first[s * ROWS : (s + 1) * ROWS])
            out = mm(fx_ref[...], jnp.concatenate([high, low, high], axis=0))
            cr, ci = out[:ROWS, :128], out[:ROWS, 128:]
            sr, si = out[ROWS:, :128], out[ROWS:, 128:]
            spec[k + s, 0, :ROWS] = cr + si
            spec[k + s, 0, ROWS:] = cr - si
            spec[k + s, 1, :ROWS] = ci - sr
            spec[k + s, 1, ROWS:] = ci + sr

    for s in range(4):
        weights(ALWAYS[s], s)
    enc_load.wait()
    count = live_lists(enc_ref, order, place, pair_c, pair_p, pair_count)
    for s in range(4):
        deposit(s)
        weights(order[4 + s], s)
    for load in loads[:2]:
        load.wait()

    def four_sources(j, _):
        k = 4 * j
        for half in (0, 2):
            spectra(k - 4 + half, (half, half + 1))
        for s in range(4):
            deposit(s)
            weights(order[k + 4 + s], s)
        return 0

    turns = (count + 3) // 4
    lax.fori_loop(1, turns, four_sources, 0)
    for half in (0, 2):
        spectra(4 * turns - 4 + half, (half, half + 1))
    for load in loads[2:]:
        load.wait()

    me = lax.axis_index("dom")
    index = lax.broadcasted_iota(jnp.int32, (ROWS, 128), 0).astype(F32)

    def multiply(target, _):
        def partner(j, add):
            c = pair_c[target * 8 + j]
            p = pair_p[target * 8 + j]
            for t in range(2 * ROWS // 16):
                rows = slice(16 * t, 16 * t + 16)
                re = spec[p, 0, rows]
                im = spec[p, 1, rows]
                for part in range(2):
                    kr = kv[c, part, 0, rows]
                    ki = kv[c, part, 1, rows]
                    real = kr * re - ki * im
                    imag = kr * im + ki * re
                    if add:
                        real = acc[target, part, 0, rows] + real
                        imag = acc[target, part, 1, rows] + imag
                    acc[target, part, 0, rows] = real
                    acc[target, part, 1, rows] = imag

        def later(j, _):
            partner(j, True)
            return 0

        @pl.when(pair_count[target] == 0)
        def _():
            acc[target] = jnp.zeros_like(acc[target])

        @pl.when(pair_count[target] > 0)
        def _():
            partner(0, False)
            lax.fori_loop(1, pair_count[target], later, 0)

        return 0

    lax.fori_loop(0, 2 * BUN, multiply, 0)

    def finish(beam, _):
        for b in range(BUN):
            target = beam * BUN + b
            stacks = []
            for part in range(2):
                rp, rm = acc[target, part, 0, :ROWS], acc[target, part, 0, ROWS:]
                ip, im = acc[target, part, 1, :ROWS], acc[target, part, 1, ROWS:]
                top = jnp.concatenate([rp + rm, ip + im], axis=1)
                low = jnp.concatenate([im - ip, rp - rm], axis=1)
                dh, dl = high_low(jnp.concatenate([top, low], axis=0))
                stacks.append(jnp.concatenate([dh, dl, dh], axis=0))
            first = mm(ix_ref[...], jnp.concatenate(stacks, axis=1))
            for part in range(2):
                rows = slice((2 * b + part) * ROWS, (2 * b + part + 1) * ROWS)
                bh_ref[rows], bl_ref[rows] = high_low(first[:, 256 * part : 256 * part + 256])
        wide = mm(bh_ref[...], iy_ref[...])
        fields = wide[:, :128] + wide[:, 128:] + mm(bl_ref[...], iy_ref[:, :128])
        for b in range(BUN):
            for part in range(2):
                for i in range(SLICES):
                    top = (2 * b + part) * ROWS + 4 * i
                    win[beam, b, i, part] = fields[top : top + G, i : i + G]
        pltpu.make_async_copy(win.at[beam], f_any.at[beam], out_sem.at[beam]).start()
        for b in range(BUN):
            x = jnp.broadcast_to(g_ref[doms + me, pl.ds(beam * 8 + b, 1), :], (ROWS, 128))
            y = jnp.broadcast_to(g_ref[doms + me, pl.ds(beam * 8 + 4 + b, 1), :], (ROWS, 128))
            weight_x = jnp.maximum(0.0, 1.0 - jnp.abs(x - index))
            yh, yl = high_low(jnp.maximum(0.0, 1.0 - jnp.abs(y - index)))
            fh, fl = high_low(fields[2 * b * ROWS : 2 * (b + 1) * ROWS, :ROWS])
            both = mm(jnp.concatenate([fh, fl], axis=0), jnp.concatenate([yh, yl], axis=1))
            sampled = both[: 2 * ROWS, :128] + both[2 * ROWS :, :128] + both[: 2 * ROWS, 128:]
            for part in range(2):
                kick_ref[part, beam, b : b + 1, :] = jnp.sum(
                    weight_x * sampled[part * ROWS : (part + 1) * ROWS], axis=0, keepdims=True
                )
        return 0

    lax.fori_loop(0, 2, finish, 0)
    kicks = pltpu.make_async_copy(kick_ref, kick_any, enc_sem)
    kicks.start()
    for beam in range(2):
        pltpu.make_async_copy(win.at[beam], f_any.at[beam], out_sem.at[beam]).wait()
    kicks.wait()


def solve(gathered, enc):
    doms, particles = gathered.shape[0] // 3, gathered.shape[2]
    vmem = pl.BlockSpec(memory_space=pltpu.VMEM)
    anywhere = pl.BlockSpec(memory_space=pl.ANY)
    consts = [jnp.asarray(t) for t in tables(CHARGE / (particles * doms))]
    weight = pltpu.VMEM((2 * ROWS, doms * particles), BF)
    return pl.pallas_call(
        functools.partial(solve_kernel, doms),
        out_shape=(
            jax.ShapeDtypeStruct((2, BUN, SLICES, 2, G, G), F32),
            jax.ShapeDtypeStruct((2, 2, BUN, particles), F32),
        ),
        in_specs=[vmem] + [anywhere] * (1 + len(consts)),
        out_specs=(anywhere, anywhere),
        scratch_shapes=[pltpu.VMEM(t.shape, t.dtype) for t in consts] + [
            pltpu.SemaphoreType.DMA((len(consts),)),
            [weight] * 4,
            [weight] * 4,
            [pltpu.VMEM((2 * ROWS, 2 * ROWS), BF)] * 4,
            pltpu.VMEM((2 * SRC + 4, 2, 2 * ROWS, 128), F32),
            pltpu.VMEM((2 * BUN, 2, 2, 2 * ROWS, 128), F32),
            pltpu.VMEM((BUN * 2 * ROWS, 256), BF),
            pltpu.VMEM((BUN * 2 * ROWS, 256), BF),
            pltpu.VMEM((2, BUN, SLICES, 2, G, G), F32),
            pltpu.VMEM((2, 2, BUN, particles), F32),
            pltpu.SMEM((3, 8, 128), jnp.int32),
            pltpu.SMEM((2 * SRC + 8,), jnp.int32),
            pltpu.SMEM((2 * SRC,), jnp.int32),
            pltpu.SMEM((2 * BUN * 8,), jnp.int32),
            pltpu.SMEM((2 * BUN * 8,), jnp.int32),
            pltpu.SMEM((2 * BUN,), jnp.int32),
            pltpu.SemaphoreType.DMA,
            pltpu.SemaphoreType.DMA((2,)),
        ],
        compiler_params=pltpu.CompilerParams(vmem_limit_bytes=24 * 1024 * 1024),
        name="solve",
    )(gathered, enc, *[pltpu.with_memory_space_constraint(t, pltpu.HBM) for t in consts])


def on_device(positions, slice_index, encounters):
    groups, doms = lax.axis_size("bunch"), lax.axis_size("dom")
    particles = positions.shape[3]
    anywhere = pl.BlockSpec(memory_space=pl.ANY)
    gathered, enc = pl.pallas_call(
        functools.partial(exchange_kernel, groups, doms),
        out_shape=(
            jax.ShapeDtypeStruct((3 * doms, 16, particles), F32),
            jax.ShapeDtypeStruct((3, 8, 128), jnp.int32),
        ),
        in_specs=[anywhere] * 3,
        out_specs=(anywhere, anywhere),
        scratch_shapes=[
            pltpu.VMEM(positions.shape, F32),
            pltpu.VMEM(slice_index.shape, jnp.int32),
            pltpu.VMEM(encounters.shape, jnp.int32),
            pltpu.VMEM((16, particles), F32),
            pltpu.VMEM((8, 128), jnp.int32),
            pltpu.SemaphoreType.DMA((3,)),
            pltpu.SemaphoreType.DMA((4,)),
        ],
        compiler_params=pltpu.CompilerParams(
            collective_id=0, has_side_effects=True, vmem_limit_bytes=1024 * 1024
        ),
        name="exchange",
    )(*[pltpu.with_memory_space_constraint(v, pltpu.HBM) for v in (positions, slice_index, encounters)])
    return solve(gathered, enc)


def solution(mesh):
    placed = (P(None, None, "bunch", "dom"), P(None, "bunch", "dom"), P("bunch", None))
    return jax.shard_map(
        on_device,
        mesh=mesh,
        in_specs=placed,
        out_specs=(P(None, "bunch", None, None, None, None), P(None, None, "bunch", "dom")),
        check_vma=False,
    )
```

```python
import functools

import jax
import jax.numpy as jnp
import ml_dtypes
import numpy as np
from jax import lax
from jax.experimental import pallas as pl
from jax.experimental.pallas import tpu as pltpu
from jax.sharding import PartitionSpec as P

G = 64
SLICES = 4
R = 3
NOFF = 7
CHARGE = 8.0
SOFTEN = 1.0

BUN = 4
SRC = BUN + 2 * R
ALWAYS = (SRC, 2 * SRC - 1, R - 1, R + BUN)
N1 = 152
N2 = 134
ROWS = 80
MESH = pl.DeviceIdType.MESH
BF = jnp.bfloat16
F32 = jnp.float32


def split_table(values):
    high = values.astype(ml_dtypes.bfloat16)
    low = (values - high.astype(np.float64)).astype(ml_dtypes.bfloat16)
    return high, low


@functools.lru_cache(maxsize=None)
def tables(scale):
    line = np.arange(ROWS)
    kx = np.arange(ROWS)
    live_kx = (kx <= N1 // 2).astype(np.float64)
    ky = np.arange(128)
    live_ky = (ky <= N2 // 2).astype(np.float64)

    phase_y = 2.0 * np.pi * (line[:, None] * ky[None, :] % N2) / N2
    along = np.concatenate([np.cos(phase_y) * live_ky, -np.sin(phase_y) * live_ky], axis=1)
    high, low = split_table(along)
    fwd_y = np.concatenate([np.concatenate([high, high], axis=0), np.concatenate([low, low], axis=0)], axis=1)

    phase_x = 2.0 * np.pi * (kx[:, None] * line[None, :] % N1) / N1
    cos_x = np.cos(phase_x) * live_kx[:, None]
    sin_x = np.sin(phase_x) * live_kx[:, None]
    high, low = split_table(np.concatenate([cos_x, sin_x], axis=0))
    fwd_x = np.concatenate([high, high, low], axis=1)

    half = np.where((kx == 0) | (kx == N1 // 2), 0.5, 1.0) / (N1 * N2)
    high, low = split_table(np.concatenate([(cos_x * half[:, None]).T, (sin_x * half[:, None]).T], axis=1))
    inv_x = np.concatenate([high, high, low], axis=1)

    twice = np.where((ky == 0) | (ky == N2 // 2), 1.0, 2.0) * live_ky
    cell = np.arange(128)
    live_cell = (cell < G + SLICES - 1).astype(np.float64)
    phase = 2.0 * np.pi * (ky[:, None] * cell[None, :] % N2) / N2
    back = np.concatenate([np.cos(phase) * twice[:, None], -np.sin(phase) * twice[:, None]], axis=0)
    inv_y = np.concatenate(split_table(back * live_cell[None, :]), axis=1)

    d1 = np.arange(N1)
    d1 = np.where(d1 < N1 // 2, d1, d1 - N1).astype(np.float64)
    d2 = np.arange(N2)
    d2 = np.where(d2 < N2 // 2, d2, d2 - N2).astype(np.float64)
    spectra = np.zeros((NOFF, 2, 2, 2 * ROWS, 128), np.float32)
    rows = np.arange(N1 // 2 + 1)
    for column in range(NOFF):
        along_x = d1[:, None] + 20.0 * (column - R)
        along_y = d2[None, :] + 3.0 * (column - R)
        spread = along_x * along_x + along_y * along_y + SOFTEN
        for part, value in enumerate((along_x / spread, along_y / spread)):
            hat = np.fft.fft2(value)[:, : N2 // 2 + 1] * scale
            for half_index, pick in enumerate((rows, (-rows) % N1)):
                place = slice(half_index * ROWS, half_index * ROWS + rows.size)
                spectra[column, part, 0, place, : N2 // 2 + 1] = hat[pick].real
                spectra[column, part, 1, place, : N2 // 2 + 1] = hat[pick].imag
    return fwd_y, fwd_x, inv_x, inv_y, spectra


def exchange_kernel(
    groups, doms,
    pos_any, sl_any, enc_any, g_ref, e_ref,
    pos_ref, sl_ref, enc_ref, block, encs, in_sem, sems,
):
    n = lax.axis_index("bunch")
    me = lax.axis_index("dom")
    loads = [
        pltpu.make_async_copy(src, dst, in_sem.at[k])
        for k, (src, dst) in enumerate(((pos_any, pos_ref), (sl_any, sl_ref), (enc_any, enc_ref)))
    ]
    for load in loads:
        load.start()
    peers = []
    for off in (1, -1, 0):
        for j in range(doms):
            if off == 0 and j == 0:
                continue
            peers.append((off, lax.rem(n + off + groups, groups), lax.rem(me + j, doms)))

    barrier = pltpu.get_barrier_semaphore()
    for _, there, dom in peers:
        pl.semaphore_signal(barrier, inc=1, device_id=(there, dom), device_id_type=MESH)

    for load in loads:
        load.wait()
    centre = 0.5 * (G - 1)
    for beam in range(2):
        gap = sl_ref[beam].astype(F32)
        block[beam * 8 : beam * 8 + 4, :] = (centre + pos_ref[0, beam]) + 4.0 * gap
        block[beam * 8 + 4 : beam * 8 + 8, :] = (centre + pos_ref[1, beam]) + gap
    encs[...] = jnp.zeros_like(encs)
    encs[0:BUN, 0:NOFF] = enc_ref[...]
    pl.semaphore_wait(barrier, len(peers))

    for off in (1, -1):
        pltpu.make_async_remote_copy(
            src_ref=encs,
            dst_ref=e_ref.at[1 - off],
            send_sem=sems.at[0],
            recv_sem=sems.at[1],
            device_id=(lax.rem(n + off + groups, groups), me),
            device_id_type=MESH,
        ).start()
    for off, there, dom in peers:
        pltpu.make_async_remote_copy(
            src_ref=block,
            dst_ref=g_ref.at[(1 - off) * doms + me],
            send_sem=sems.at[2],
            recv_sem=sems.at[3],
            device_id=(there, dom),
            device_id_type=MESH,
        ).start()
    pltpu.make_async_copy(encs, e_ref.at[1], sems.at[1]).start()
    pltpu.make_async_copy(block, g_ref.at[doms + me], sems.at[3]).start()
    for sem, ref in ((3, g_ref), (1, e_ref), (2, g_ref.at[pl.ds(0, len(peers))]), (0, e_ref.at[pl.ds(0, 2)])):
        pltpu.make_async_copy(ref, ref, sems.at[sem]).wait()


def high_low(values):
    high = values.astype(BF)
    return high, (values - high.astype(F32)).astype(BF)


def mm(a, b):
    return jnp.dot(a, b, preferred_element_type=F32)


def live_lists(enc_ref, order, place, pair_c, pair_p, pair_count):
    flags = []
    for beam in range(2):
        for b in range(BUN):
            row = []
            for c in range(NOFF):
                if beam == 0:
                    row.append(enc_ref[1, b, c])
                else:
                    a = b + c + 1
                    row.append(enc_ref[a // BUN, a % BUN, 2 * R - c])
            flags.append(row)
    count = jnp.int32(0)
    for k in range(2 * SRC + 8):
        order[k] = 0
    for source in ALWAYS:
        place[source] = count
        order[count] = source
        count = count + 1
    for source in range(2 * SRC):
        if source in ALWAYS:
            continue
        beam, m = source // SRC, source % SRC
        users = [flags[(1 - beam) * BUN + b][m - b] for b in range(BUN) if 0 <= m - b < NOFF]
        need = users[0]
        for other in users[1:]:
            need = jnp.maximum(need, other)
        order[count] = source
        place[source] = count
        count = count + need
    order[count] = 0
    for target in range(2 * BUN):
        beam, b = target // BUN, target % BUN
        total = jnp.int32(0)
        for c in range(NOFF):
            pair_c[target * 8 + total] = c
            pair_p[target * 8 + total] = place[(1 - beam) * SRC + b + c]
            total = total + flags[target][c]
        pair_count[target] = total
    return count


def solve_kernel(
    doms,
    g_ref, enc_any, fy_any, fx_any, ix_any, iy_any, kv_any,
    f_any, kick_any,
    fy_ref, fx_ref, ix_ref, iy_ref, kv, table_sem,
    q, wx, wy, grids, spec, acc, bh_ref, bl_ref, win, kick_ref,
    enc_ref, order, place, pair_c, pair_p, pair_count, enc_sem, out_sem,
):
    enc_load = pltpu.make_async_copy(enc_any, enc_ref, enc_sem)
    enc_load.start()
    pairs = ((fy_any, fy_ref), (fx_any, fx_ref), (kv_any, kv), (ix_any, ix_ref), (iy_any, iy_ref))
    loads = [pltpu.make_async_copy(src, dst, table_sem.at[k]) for k, (src, dst) in enumerate(pairs)]
    for load in loads:
        load.start()

    where_at = g_ref[...]
    cell = jnp.floor(where_at)
    upper = where_at - cell
    q[0] = cell
    for slot, part in ((1, 1.0 - upper), (3, upper)):
        high = part.astype(BF).astype(F32)
        q[slot] = high
        q[slot + 1] = part - high

    line = lax.broadcasted_iota(jnp.int32, (16, 128), 0).astype(F32)
    lines = [(line + 16.0 * t).astype(BF) for t in range(ROWS // 16)]
    below = [(line + (16.0 * t - 1.0)).astype(BF) for t in range(ROWS // 16)]
    nothing = jnp.zeros((16, 128), BF)

    def weights(source, slot):
        beam = source // SRC
        m = source - beam * SRC
        grp = (m + 1) // BUN
        bunch = (m + 1) % BUN
        for coord, dest in ((0, wx[slot]), (1, wy[slot])):
            row = beam * 8 + coord * 4 + bunch
            for d in range(doms):
                cells, lh, ll, uh, ul = [
                    jnp.broadcast_to(q[j, grp * doms + d, pl.ds(row, 1), :], (16, 128)).astype(BF) for j in range(5)
                ]
                cols = slice(d * 128, (d + 1) * 128)
                for t in range(ROWS // 16):
                    first = lines[t] == cells
                    second = below[t] == cells
                    dest[16 * t : 16 * t + 16, cols] = jnp.where(first, lh, jnp.where(second, uh, nothing))
                    dest[ROWS + 16 * t : ROWS + 16 * t + 16, cols] = jnp.where(
                        first, ll, jnp.where(second, ul, nothing)
                    )

    def deposit(slot):
        both = lax.dot_general(
            wx[slot][...], wy[slot][...], (((1,), (1,)), ((), ())), preferred_element_type=F32
        )
        high, low = high_low(both[:ROWS] + both[ROWS:])
        grids[slot][:ROWS] = high
        grids[slot][ROWS:] = low

    def spectra(k, slots):
        grid = [grids[slot][:ROWS] for slot in slots]
        wide = len(slots) * ROWS
        low = [grids[slot][ROWS:] for slot in slots]
        first = mm(jnp.concatenate(grid + low, axis=0), fy_ref[:, :256])
        first = first[:wide] + first[wide:] + mm(jnp.concatenate(grid, axis=0), fy_ref[:, 256:])
        for s in range(len(slots)):
            high, low = high_low(first[s * ROWS : (s + 1) * ROWS])
            out = mm(fx_ref[...], jnp.concatenate([high, low, high], axis=0))
            cr, ci = out[:ROWS, :128], out[:ROWS, 128:]
            sr, si = out[ROWS:, :128], out[ROWS:, 128:]
            spec[k + s, 0, :ROWS] = cr + si
            spec[k + s, 0, ROWS:] = cr - si
            spec[k + s, 1, :ROWS] = ci - sr
            spec[k + s, 1, ROWS:] = ci + sr

    for s in range(4):
        weights(ALWAYS[s], s)
    enc_load.wait()
    count = live_lists(enc_ref, order, place, pair_c, pair_p, pair_count)
    for s in range(4):
        deposit(s)
        weights(order[4 + s], s)
    for load in loads[:2]:
        load.wait()

    def four_sources(j, _):
        k = 4 * j
        for half in (0, 2):
            spectra(k - 4 + half, (half, half + 1))
        for s in range(4):
            deposit(s)
            weights(order[k + 4 + s], s)
        return 0

    turns = (count + 3) // 4
    lax.fori_loop(1, turns, four_sources, 0)
    for half in (0, 2):
        spectra(4 * turns - 4 + half, (half, half + 1))
    for load in loads[2:]:
        load.wait()

    me = lax.axis_index("dom")
    index = lax.broadcasted_iota(jnp.int32, (ROWS, 128), 0).astype(F32)

    def multiply(target, _):
        def partner(j, add):
            c = pair_c[target * 8 + j]
            p = pair_p[target * 8 + j]
            for t in range(2 * ROWS // 16):
                rows = slice(16 * t, 16 * t + 16)
                re = spec[p, 0, rows]
                im = spec[p, 1, rows]
                for part in range(2):
                    kr = kv[c, part, 0, rows]
                    ki = kv[c, part, 1, rows]
                    real = kr * re - ki * im
                    imag = kr * im + ki * re
                    if add:
                        real = acc[target, part, 0, rows] + real
                        imag = acc[target, part, 1, rows] + imag
                    acc[target, part, 0, rows] = real
                    acc[target, part, 1, rows] = imag

        def later(j, _):
            partner(j, True)
            return 0

        @pl.when(pair_count[target] == 0)
        def _():
            acc[target] = jnp.zeros_like(acc[target])

        @pl.when(pair_count[target] > 0)
        def _():
            partner(0, False)
            lax.fori_loop(1, pair_count[target], later, 0)

        return 0

    lax.fori_loop(0, 2 * BUN, multiply, 0)

    def finish(beam, _):
        for b in range(BUN):
            target = beam * BUN + b
            stacks = []
            for part in range(2):
                rp, rm = acc[target, part, 0, :ROWS], acc[target, part, 0, ROWS:]
                ip, im = acc[target, part, 1, :ROWS], acc[target, part, 1, ROWS:]
                top = jnp.concatenate([rp + rm, ip + im], axis=1)
                low = jnp.concatenate([im - ip, rp - rm], axis=1)
                dh, dl = high_low(jnp.concatenate([top, low], axis=0))
                stacks.append(jnp.concatenate([dh, dl, dh], axis=0))
            first = mm(ix_ref[...], jnp.concatenate(stacks, axis=1))
            for part in range(2):
                rows = slice((2 * b + part) * ROWS, (2 * b + part + 1) * ROWS)
                bh_ref[rows], bl_ref[rows] = high_low(first[:, 256 * part : 256 * part + 256])
        wide = mm(bh_ref[...], iy_ref[...])
        fields = wide[:, :128] + wide[:, 128:] + mm(bl_ref[...], iy_ref[:, :128])
        for b in range(BUN):
            for part in range(2):
                for i in range(SLICES):
                    top = (2 * b + part) * ROWS + 4 * i
                    win[beam, b, i, part] = fields[top : top + G, i : i + G]
        pltpu.make_async_copy(win.at[beam], f_any.at[beam], out_sem.at[beam]).start()
        for b in range(BUN):
            x = jnp.broadcast_to(g_ref[doms + me, pl.ds(beam * 8 + b, 1), :], (ROWS, 128))
            y = jnp.broadcast_to(g_ref[doms + me, pl.ds(beam * 8 + 4 + b, 1), :], (ROWS, 128))
            weight_x = jnp.maximum(0.0, 1.0 - jnp.abs(x - index))
            yh, yl = high_low(jnp.maximum(0.0, 1.0 - jnp.abs(y - index)))
            fh, fl = high_low(fields[2 * b * ROWS : 2 * (b + 1) * ROWS, :ROWS])
            both = mm(jnp.concatenate([fh, fl], axis=0), jnp.concatenate([yh, yl], axis=1))
            sampled = both[: 2 * ROWS, :128] + both[2 * ROWS :, :128] + both[: 2 * ROWS, 128:]
            for part in range(2):
                kick_ref[part, beam, b : b + 1, :] = jnp.sum(
                    weight_x * sampled[part * ROWS : (part + 1) * ROWS], axis=0, keepdims=True
                )
        return 0

    lax.fori_loop(0, 2, finish, 0)
    kicks = pltpu.make_async_copy(kick_ref, kick_any, enc_sem)
    kicks.start()
    for beam in range(2):
        pltpu.make_async_copy(win.at[beam], f_any.at[beam], out_sem.at[beam]).wait()
    kicks.wait()


def solve(gathered, enc):
    doms, particles = gathered.shape[0] // 3, gathered.shape[2]
    vmem = pl.BlockSpec(memory_space=pltpu.VMEM)
    anywhere = pl.BlockSpec(memory_space=pl.ANY)
    consts = [jnp.asarray(t) for t in tables(CHARGE / (particles * doms))]
    weight = pltpu.VMEM((2 * ROWS, doms * particles), BF)
    return pl.pallas_call(
        functools.partial(solve_kernel, doms),
        out_shape=(
            jax.ShapeDtypeStruct((2, BUN, SLICES, 2, G, G), F32),
            jax.ShapeDtypeStruct((2, 2, BUN, particles), F32),
        ),
        in_specs=[vmem] + [anywhere] * (1 + len(consts)),
        out_specs=(anywhere, anywhere),
        scratch_shapes=[pltpu.VMEM(t.shape, t.dtype) for t in consts] + [
            pltpu.SemaphoreType.DMA((len(consts),)),
            pltpu.VMEM((5, 3 * doms, 16, particles), F32),
            [weight] * 4,
            [weight] * 4,
            [pltpu.VMEM((2 * ROWS, 2 * ROWS), BF)] * 4,
            pltpu.VMEM((2 * SRC + 4, 2, 2 * ROWS, 128), F32),
            pltpu.VMEM((2 * BUN, 2, 2, 2 * ROWS, 128), F32),
            pltpu.VMEM((BUN * 2 * ROWS, 256), BF),
            pltpu.VMEM((BUN * 2 * ROWS, 256), BF),
            pltpu.VMEM((2, BUN, SLICES, 2, G, G), F32),
            pltpu.VMEM((2, 2, BUN, particles), F32),
            pltpu.SMEM((3, 8, 128), jnp.int32),
            pltpu.SMEM((2 * SRC + 8,), jnp.int32),
            pltpu.SMEM((2 * SRC,), jnp.int32),
            pltpu.SMEM((2 * BUN * 8,), jnp.int32),
            pltpu.SMEM((2 * BUN * 8,), jnp.int32),
            pltpu.SMEM((2 * BUN,), jnp.int32),
            pltpu.SemaphoreType.DMA,
            pltpu.SemaphoreType.DMA((2,)),
        ],
        compiler_params=pltpu.CompilerParams(vmem_limit_bytes=24 * 1024 * 1024),
        name="solve",
    )(gathered, enc, *[pltpu.with_memory_space_constraint(t, pltpu.HBM) for t in consts])


def on_device(positions, slice_index, encounters):
    groups, doms = lax.axis_size("bunch"), lax.axis_size("dom")
    particles = positions.shape[3]
    anywhere = pl.BlockSpec(memory_space=pl.ANY)
    gathered, enc = pl.pallas_call(
        functools.partial(exchange_kernel, groups, doms),
        out_shape=(
            jax.ShapeDtypeStruct((3 * doms, 16, particles), F32),
            jax.ShapeDtypeStruct((3, 8, 128), jnp.int32),
        ),
        in_specs=[anywhere] * 3,
        out_specs=(anywhere, anywhere),
        scratch_shapes=[
            pltpu.VMEM(positions.shape, F32),
            pltpu.VMEM(slice_index.shape, jnp.int32),
            pltpu.VMEM(encounters.shape, jnp.int32),
            pltpu.VMEM((16, particles), F32),
            pltpu.VMEM((8, 128), jnp.int32),
            pltpu.SemaphoreType.DMA((3,)),
            pltpu.SemaphoreType.DMA((4,)),
        ],
        compiler_params=pltpu.CompilerParams(
            collective_id=0, has_side_effects=True, vmem_limit_bytes=1024 * 1024
        ),
        name="exchange",
    )(*[pltpu.with_memory_space_constraint(v, pltpu.HBM) for v in (positions, slice_index, encounters)])
    return solve(gathered, enc)


def solution(mesh):
    placed = (P(None, None, "bunch", "dom"), P(None, "bunch", "dom"), P("bunch", None))
    return jax.shard_map(
        on_device,
        mesh=mesh,
        in_specs=placed,
        out_specs=(P(None, "bunch", None, None, None, None), P(None, None, "bunch", "dom")),
        check_vma=False,
    )
```

```python
import functools

import jax
import jax.numpy as jnp
import ml_dtypes
import numpy as np
from jax import lax
from jax.experimental import pallas as pl
from jax.experimental.pallas import tpu as pltpu
from jax.sharding import PartitionSpec as P

G = 64
SLICES = 4
R = 3
NOFF = 7
CHARGE = 8.0
SOFTEN = 1.0

BUN = 4
SRC = BUN + 2 * R
ALWAYS = (SRC, 2 * SRC - 1, R - 1, R + BUN)
N1 = 152
N2 = 134
ROWS = 80
MESH = pl.DeviceIdType.MESH
BF = jnp.bfloat16
F32 = jnp.float32


def split_table(values):
    high = values.astype(ml_dtypes.bfloat16)
    low = (values - high.astype(np.float64)).astype(ml_dtypes.bfloat16)
    return high, low


@functools.lru_cache(maxsize=None)
def tables(scale):
    line = np.arange(ROWS)
    kx = np.arange(ROWS)
    live_kx = (kx <= N1 // 2).astype(np.float64)
    ky = np.arange(128)
    live_ky = (ky <= N2 // 2).astype(np.float64)

    phase_y = 2.0 * np.pi * (line[:, None] * ky[None, :] % N2) / N2
    along = np.concatenate([np.cos(phase_y) * live_ky, -np.sin(phase_y) * live_ky], axis=1)
    high, low = split_table(along)
    fwd_y = np.concatenate([high, high, low], axis=0)

    phase_x = 2.0 * np.pi * (kx[:, None] * line[None, :] % N1) / N1
    cos_x = np.cos(phase_x) * live_kx[:, None]
    sin_x = np.sin(phase_x) * live_kx[:, None]
    high, low = split_table(np.concatenate([cos_x, sin_x], axis=0))
    fwd_x = np.concatenate([high, high, low], axis=1)

    half = np.where((kx == 0) | (kx == N1 // 2), 0.5, 1.0) / (N1 * N2)
    high, low = split_table(np.concatenate([(cos_x * half[:, None]).T, (sin_x * half[:, None]).T], axis=1))
    inv_x = np.concatenate([high, high, low], axis=1)

    twice = np.where((ky == 0) | (ky == N2 // 2), 1.0, 2.0) * live_ky
    cell = np.arange(128)
    live_cell = (cell < G + SLICES - 1).astype(np.float64)
    phase = 2.0 * np.pi * (ky[:, None] * cell[None, :] % N2) / N2
    back = np.concatenate([np.cos(phase) * twice[:, None], -np.sin(phase) * twice[:, None]], axis=0)
    inv_y = np.concatenate(split_table(back * live_cell[None, :]), axis=1)

    d1 = np.arange(N1)
    d1 = np.where(d1 < N1 // 2, d1, d1 - N1).astype(np.float64)
    d2 = np.arange(N2)
    d2 = np.where(d2 < N2 // 2, d2, d2 - N2).astype(np.float64)
    spectra = np.zeros((NOFF, 2, 2, 2 * ROWS, 128), np.float32)
    rows = np.arange(N1 // 2 + 1)
    for column in range(NOFF):
        along_x = d1[:, None] + 20.0 * (column - R)
        along_y = d2[None, :] + 3.0 * (column - R)
        spread = along_x * along_x + along_y * along_y + SOFTEN
        for part, value in enumerate((along_x / spread, along_y / spread)):
            hat = np.fft.fft2(value)[:, : N2 // 2 + 1] * scale
            for half_index, pick in enumerate((rows, (-rows) % N1)):
                place = slice(half_index * ROWS, half_index * ROWS + rows.size)
                spectra[column, part, 0, place, : N2 // 2 + 1] = hat[pick].real
                spectra[column, part, 1, place, : N2 // 2 + 1] = hat[pick].imag
    return fwd_y, fwd_x, inv_x, inv_y, spectra


def exchange_kernel(
    groups, doms,
    pos_any, sl_any, enc_any, g_ref, e_ref,
    pos_ref, sl_ref, enc_ref, block, encs, in_sem, sems,
):
    n = lax.axis_index("bunch")
    me = lax.axis_index("dom")
    loads = [
        pltpu.make_async_copy(src, dst, in_sem.at[k])
        for k, (src, dst) in enumerate(((pos_any, pos_ref), (sl_any, sl_ref), (enc_any, enc_ref)))
    ]
    for load in loads:
        load.start()
    peers = []
    for off in (1, -1, 0):
        for j in range(doms):
            if off == 0 and j == 0:
                continue
            peers.append((off, lax.rem(n + off + groups, groups), lax.rem(me + j, doms)))

    barrier = pltpu.get_barrier_semaphore()
    for _, there, dom in peers:
        pl.semaphore_signal(barrier, inc=1, device_id=(there, dom), device_id_type=MESH)

    for load in loads:
        load.wait()
    centre = 0.5 * (G - 1)
    for beam in range(2):
        gap = sl_ref[beam].astype(F32)
        block[beam * 8 : beam * 8 + 4, :] = (centre + pos_ref[0, beam]) + 4.0 * gap
        block[beam * 8 + 4 : beam * 8 + 8, :] = (centre + pos_ref[1, beam]) + gap
    encs[...] = jnp.zeros_like(encs)
    encs[0:BUN, 0:NOFF] = enc_ref[...]
    pl.semaphore_wait(barrier, len(peers))

    for off in (1, -1):
        pltpu.make_async_remote_copy(
            src_ref=encs,
            dst_ref=e_ref.at[1 - off],
            send_sem=sems.at[0],
            recv_sem=sems.at[1],
            device_id=(lax.rem(n + off + groups, groups), me),
            device_id_type=MESH,
        ).start()
    for off, there, dom in peers:
        pltpu.make_async_remote_copy(
            src_ref=block,
            dst_ref=g_ref.at[(1 - off) * doms + me],
            send_sem=sems.at[2],
            recv_sem=sems.at[3],
            device_id=(there, dom),
            device_id_type=MESH,
        ).start()
    pltpu.make_async_copy(encs, e_ref.at[1], sems.at[1]).start()
    pltpu.make_async_copy(block, g_ref.at[doms + me], sems.at[3]).start()
    for sem, ref in ((3, g_ref), (1, e_ref), (2, g_ref.at[pl.ds(0, len(peers))]), (0, e_ref.at[pl.ds(0, 2)])):
        pltpu.make_async_copy(ref, ref, sems.at[sem]).wait()


def high_low(values):
    high = values.astype(BF)
    return high, (values - high.astype(F32)).astype(BF)


def mm(a, b):
    return jnp.dot(a, b, preferred_element_type=F32)


def live_lists(enc_ref, order, place, pair_c, pair_p, pair_count):
    flags = []
    for beam in range(2):
        for b in range(BUN):
            row = []
            for c in range(NOFF):
                if beam == 0:
                    row.append(enc_ref[1, b, c])
                else:
                    a = b + c + 1
                    row.append(enc_ref[a // BUN, a % BUN, 2 * R - c])
            flags.append(row)
    count = jnp.int32(0)
    for k in range(2 * SRC + 8):
        order[k] = 0
    for source in ALWAYS:
        place[source] = count
        order[count] = source
        count = count + 1
    for source in range(2 * SRC):
        if source in ALWAYS:
            continue
        beam, m = source // SRC, source % SRC
        users = [flags[(1 - beam) * BUN + b][m - b] for b in range(BUN) if 0 <= m - b < NOFF]
        need = users[0]
        for other in users[1:]:
            need = jnp.maximum(need, other)
        order[count] = source
        place[source] = count
        count = count + need
    order[count] = 0
    for target in range(2 * BUN):
        beam, b = target // BUN, target % BUN
        total = jnp.int32(0)
        for c in range(NOFF):
            pair_c[target * 8 + total] = c
            pair_p[target * 8 + total] = place[(1 - beam) * SRC + b + c]
            total = total + flags[target][c]
        pair_count[target] = total
    return count


def solve_kernel(
    doms,
    g_ref, enc_any, fy_any, fx_any, ix_any, iy_any, kv_any,
    f_any, kick_any,
    fy_ref, fx_ref, ix_ref, iy_ref, kv, table_sem,
    q, wx, wy, grids, spec, acc, bh_ref, bl_ref, win, kick_ref,
    enc_ref, order, place, pair_c, pair_p, pair_count, enc_sem, out_sem,
):
    enc_load = pltpu.make_async_copy(enc_any, enc_ref, enc_sem)
    enc_load.start()
    pairs = ((fy_any, fy_ref), (fx_any, fx_ref), (kv_any, kv), (ix_any, ix_ref), (iy_any, iy_ref))
    loads = [pltpu.make_async_copy(src, dst, table_sem.at[k]) for k, (src, dst) in enumerate(pairs)]
    for load in loads:
        load.start()

    where_at = g_ref[...]
    cell = jnp.floor(where_at)
    upper = where_at - cell
    q[0] = cell
    for slot, part in ((1, 1.0 - upper), (3, upper)):
        high = part.astype(BF).astype(F32)
        q[slot] = high
        q[slot + 1] = part - high

    line = lax.broadcasted_iota(jnp.int32, (16, 128), 0).astype(F32)
    lines = [(line + 16.0 * t).astype(BF) for t in range(ROWS // 16)]
    below = [(line + (16.0 * t - 1.0)).astype(BF) for t in range(ROWS // 16)]
    nothing = jnp.zeros((16, 128), BF)

    def weights(source, slot):
        beam = source // SRC
        m = source - beam * SRC
        grp = (m + 1) // BUN
        bunch = (m + 1) % BUN
        for coord, dest in ((0, wx[slot]), (1, wy[slot])):
            row = beam * 8 + coord * 4 + bunch
            for d in range(doms):
                cells, lh, ll, uh, ul = [
                    jnp.broadcast_to(q[j, grp * doms + d, pl.ds(row, 1), :], (16, 128)).astype(BF) for j in range(5)
                ]
                cols = slice(d * 128, (d + 1) * 128)
                for t in range(ROWS // 16):
                    first = lines[t] == cells
                    second = below[t] == cells
                    dest[16 * t : 16 * t + 16, cols] = jnp.where(first, lh, jnp.where(second, uh, nothing))
                    dest[ROWS + 16 * t : ROWS + 16 * t + 16, cols] = jnp.where(
                        first, ll, jnp.where(second, ul, nothing)
                    )

    def deposit(slot):
        both = lax.dot_general(
            wx[slot][...], wy[slot][...], (((1,), (1,)), ((), ())), preferred_element_type=F32
        )
        both = both[:ROWS] + both[ROWS:]
        high, low = high_low(both[:, :ROWS] + both[:, ROWS:])
        grids[slot][...] = jnp.concatenate([high, low, high], axis=1)

    def spectra(k, slots):
        first = mm(jnp.concatenate([grids[slot][...] for slot in slots], axis=0), fy_ref[...])
        for s in range(len(slots)):
            high, low = high_low(first[s * ROWS : (s + 1) * ROWS])
            out = mm(fx_ref[...], jnp.concatenate([high, low, high], axis=0))
            cr, ci = out[:ROWS, :128], out[:ROWS, 128:]
            sr, si = out[ROWS:, :128], out[ROWS:, 128:]
            spec[k + s, 0, :ROWS] = cr + si
            spec[k + s, 0, ROWS:] = cr - si
            spec[k + s, 1, :ROWS] = ci - sr
            spec[k + s, 1, ROWS:] = ci + sr

    for s in range(4):
        weights(ALWAYS[s], s)
    enc_load.wait()
    count = live_lists(enc_ref, order, place, pair_c, pair_p, pair_count)
    for s in range(4):
        deposit(s)
        weights(order[4 + s], s)
    for load in loads[:2]:
        load.wait()

    def four_sources(j, _):
        k = 4 * j
        for half in (0, 2):
            spectra(k - 4 + half, (half, half + 1))
        for s in range(4):
            deposit(s)
            weights(order[k + 4 + s], s)
        return 0

    turns = (count + 1) // 4
    lax.fori_loop(1, turns, four_sources, 0)

    @pl.when(count > 4 * turns)
    def _():
        for half in (0, 2):
            spectra(4 * turns - 4 + half, (half, half + 1))
        for s in range(2):
            deposit(s)
        spectra(4 * turns, (0, 1))

    @pl.when(count <= 4 * turns)
    def _():
        for half in (0, 2):
            spectra(4 * turns - 4 + half, (half, half + 1))

    for load in loads[2:]:
        load.wait()

    me = lax.axis_index("dom")
    index = lax.broadcasted_iota(jnp.int32, (ROWS, 128), 0).astype(F32)

    def multiply(target, _):
        def partner(j, add):
            c = pair_c[target * 8 + j]
            p = pair_p[target * 8 + j]
            for t in range(2 * ROWS // 16):
                rows = slice(16 * t, 16 * t + 16)
                re = spec[p, 0, rows]
                im = spec[p, 1, rows]
                for part in range(2):
                    kr = kv[c, part, 0, rows]
                    ki = kv[c, part, 1, rows]
                    real = kr * re - ki * im
                    imag = kr * im + ki * re
                    if add:
                        real = acc[target, part, 0, rows] + real
                        imag = acc[target, part, 1, rows] + imag
                    acc[target, part, 0, rows] = real
                    acc[target, part, 1, rows] = imag

        def later(j, _):
            partner(j, True)
            return 0

        @pl.when(pair_count[target] == 0)
        def _():
            acc[target] = jnp.zeros_like(acc[target])

        @pl.when(pair_count[target] > 0)
        def _():
            partner(0, False)
            lax.fori_loop(1, pair_count[target], later, 0)

        return 0

    lax.fori_loop(0, 2 * BUN, multiply, 0)

    def finish(beam, _):
        for b in range(BUN):
            target = beam * BUN + b
            stacks = []
            for part in range(2):
                rp, rm = acc[target, part, 0, :ROWS], acc[target, part, 0, ROWS:]
                ip, im = acc[target, part, 1, :ROWS], acc[target, part, 1, ROWS:]
                top = jnp.concatenate([rp + rm, ip + im], axis=1)
                low = jnp.concatenate([im - ip, rp - rm], axis=1)
                dh, dl = high_low(jnp.concatenate([top, low], axis=0))
                stacks.append(jnp.concatenate([dh, dl, dh], axis=0))
            first = mm(ix_ref[...], jnp.concatenate(stacks, axis=1))
            for part in range(2):
                rows = slice((2 * b + part) * ROWS, (2 * b + part + 1) * ROWS)
                bh_ref[rows], bl_ref[rows] = high_low(first[:, 256 * part : 256 * part + 256])
        wide = mm(bh_ref[...], iy_ref[...])
        fields = wide[:, :128] + wide[:, 128:] + mm(bl_ref[...], iy_ref[:, :128])
        for b in range(BUN):
            for part in range(2):
                for i in range(SLICES):
                    top = (2 * b + part) * ROWS + 4 * i
                    win[beam, b, i, part] = fields[top : top + G, i : i + G]
        pltpu.make_async_copy(win.at[beam], f_any.at[beam], out_sem.at[beam]).start()
        for b in range(BUN):
            x = jnp.broadcast_to(g_ref[doms + me, pl.ds(beam * 8 + b, 1), :], (ROWS, 128))
            y = jnp.broadcast_to(g_ref[doms + me, pl.ds(beam * 8 + 4 + b, 1), :], (ROWS, 128))
            weight_x = jnp.maximum(0.0, 1.0 - jnp.abs(x - index))
            yh, yl = high_low(jnp.maximum(0.0, 1.0 - jnp.abs(y - index)))
            fh, fl = high_low(fields[2 * b * ROWS : 2 * (b + 1) * ROWS, :ROWS])
            both = mm(jnp.concatenate([fh, fl], axis=0), jnp.concatenate([yh, yl], axis=1))
            sampled = both[: 2 * ROWS, :128] + both[2 * ROWS :, :128] + both[: 2 * ROWS, 128:]
            for part in range(2):
                kick_ref[part, beam, b : b + 1, :] = jnp.sum(
                    weight_x * sampled[part * ROWS : (part + 1) * ROWS], axis=0, keepdims=True
                )
        return 0

    lax.fori_loop(0, 2, finish, 0)
    kicks = pltpu.make_async_copy(kick_ref, kick_any, enc_sem)
    kicks.start()
    for beam in range(2):
        pltpu.make_async_copy(win.at[beam], f_any.at[beam], out_sem.at[beam]).wait()
    kicks.wait()


def solve(gathered, enc):
    doms, particles = gathered.shape[0] // 3, gathered.shape[2]
    vmem = pl.BlockSpec(memory_space=pltpu.VMEM)
    anywhere = pl.BlockSpec(memory_space=pl.ANY)
    consts = [jnp.asarray(t) for t in tables(CHARGE / (particles * doms))]
    weight = pltpu.VMEM((2 * ROWS, doms * particles), BF)
    return pl.pallas_call(
        functools.partial(solve_kernel, doms),
        out_shape=(
            jax.ShapeDtypeStruct((2, BUN, SLICES, 2, G, G), F32),
            jax.ShapeDtypeStruct((2, 2, BUN, particles), F32),
        ),
        in_specs=[vmem] + [anywhere] * (1 + len(consts)),
        out_specs=(anywhere, anywhere),
        scratch_shapes=[pltpu.VMEM(t.shape, t.dtype) for t in consts] + [
            pltpu.SemaphoreType.DMA((len(consts),)),
            pltpu.VMEM((5, 3 * doms, 16, particles), F32),
            [weight] * 4,
            [weight] * 4,
            [pltpu.VMEM((ROWS, 3 * ROWS), BF)] * 4,
            pltpu.VMEM((2 * SRC + 4, 2, 2 * ROWS, 128), F32),
            pltpu.VMEM((2 * BUN, 2, 2, 2 * ROWS, 128), F32),
            pltpu.VMEM((BUN * 2 * ROWS, 256), BF),
            pltpu.VMEM((BUN * 2 * ROWS, 256), BF),
            pltpu.VMEM((2, BUN, SLICES, 2, G, G), F32),
            pltpu.VMEM((2, 2, BUN, particles), F32),
            pltpu.SMEM((3, 8, 128), jnp.int32),
            pltpu.SMEM((2 * SRC + 8,), jnp.int32),
            pltpu.SMEM((2 * SRC,), jnp.int32),
            pltpu.SMEM((2 * BUN * 8,), jnp.int32),
            pltpu.SMEM((2 * BUN * 8,), jnp.int32),
            pltpu.SMEM((2 * BUN,), jnp.int32),
            pltpu.SemaphoreType.DMA,
            pltpu.SemaphoreType.DMA((2,)),
        ],
        compiler_params=pltpu.CompilerParams(vmem_limit_bytes=24 * 1024 * 1024),
        name="solve",
    )(gathered, enc, *[pltpu.with_memory_space_constraint(t, pltpu.HBM) for t in consts])


def on_device(positions, slice_index, encounters):
    groups, doms = lax.axis_size("bunch"), lax.axis_size("dom")
    particles = positions.shape[3]
    anywhere = pl.BlockSpec(memory_space=pl.ANY)
    gathered, enc = pl.pallas_call(
        functools.partial(exchange_kernel, groups, doms),
        out_shape=(
            jax.ShapeDtypeStruct((3 * doms, 16, particles), F32),
            jax.ShapeDtypeStruct((3, 8, 128), jnp.int32),
        ),
        in_specs=[anywhere] * 3,
        out_specs=(anywhere, anywhere),
        scratch_shapes=[
            pltpu.VMEM(positions.shape, F32),
            pltpu.VMEM(slice_index.shape, jnp.int32),
            pltpu.VMEM(encounters.shape, jnp.int32),
            pltpu.VMEM((16, particles), F32),
            pltpu.VMEM((8, 128), jnp.int32),
            pltpu.SemaphoreType.DMA((3,)),
            pltpu.SemaphoreType.DMA((4,)),
        ],
        compiler_params=pltpu.CompilerParams(
            collective_id=0, has_side_effects=True, vmem_limit_bytes=1024 * 1024
        ),
        name="exchange",
    )(*[pltpu.with_memory_space_constraint(v, pltpu.HBM) for v in (positions, slice_index, encounters)])
    return solve(gathered, enc)


def solution(mesh):
    placed = (P(None, None, "bunch", "dom"), P(None, "bunch", "dom"), P("bunch", None))
    return jax.shard_map(
        on_device,
        mesh=mesh,
        in_specs=placed,
        out_specs=(P(None, "bunch", None, None, None, None), P(None, None, "bunch", "dom")),
        check_vma=False,
    )
```

```python
import functools

import jax
import jax.numpy as jnp
import ml_dtypes
import numpy as np
from jax import lax
from jax.experimental import pallas as pl
from jax.experimental.pallas import tpu as pltpu
from jax.sharding import PartitionSpec as P

G = 64
SLICES = 4
R = 3
NOFF = 7
CHARGE = 8.0
SOFTEN = 1.0

BUN = 4
SRC = BUN + 2 * R
ALWAYS = (SRC, 2 * SRC - 1, R - 1, R + BUN)
N1 = 152
N2 = 134
ROWS = 80
MESH = pl.DeviceIdType.MESH
BF = jnp.bfloat16
F32 = jnp.float32


def split_table(values):
    high = values.astype(ml_dtypes.bfloat16)
    low = (values - high.astype(np.float64)).astype(ml_dtypes.bfloat16)
    return high, low


@functools.lru_cache(maxsize=None)
def tables(scale):
    line = np.arange(ROWS)
    kx = np.arange(ROWS)
    live_kx = (kx <= N1 // 2).astype(np.float64)
    ky = np.arange(128)
    live_ky = (ky <= N2 // 2).astype(np.float64)

    phase_y = 2.0 * np.pi * (line[:, None] * ky[None, :] % N2) / N2
    along = np.concatenate([np.cos(phase_y) * live_ky, -np.sin(phase_y) * live_ky], axis=1)
    high, low = split_table(along)
    fwd_y = np.concatenate([high, high, low], axis=0)

    phase_x = 2.0 * np.pi * (kx[:, None] * line[None, :] % N1) / N1
    cos_x = np.cos(phase_x) * live_kx[:, None]
    sin_x = np.sin(phase_x) * live_kx[:, None]
    high, low = split_table(np.concatenate([cos_x, sin_x], axis=0))
    fwd_x = np.concatenate([high, high, low], axis=1)

    half = np.where((kx == 0) | (kx == N1 // 2), 0.5, 1.0) / (N1 * N2)
    high, low = split_table(np.concatenate([(cos_x * half[:, None]).T, (sin_x * half[:, None]).T], axis=1))
    inv_x = np.concatenate([high, high, low], axis=1)

    twice = np.where((ky == 0) | (ky == N2 // 2), 1.0, 2.0) * live_ky
    cell = np.arange(128)
    live_cell = (cell < G + SLICES - 1).astype(np.float64)
    phase = 2.0 * np.pi * (ky[:, None] * cell[None, :] % N2) / N2
    back = np.concatenate([np.cos(phase) * twice[:, None], -np.sin(phase) * twice[:, None]], axis=0)
    inv_y = np.concatenate(split_table(back * live_cell[None, :]), axis=1)

    d1 = np.arange(N1)
    d1 = np.where(d1 < N1 // 2, d1, d1 - N1).astype(np.float64)
    d2 = np.arange(N2)
    d2 = np.where(d2 < N2 // 2, d2, d2 - N2).astype(np.float64)
    spectra = np.zeros((NOFF, 2, 2, 2 * ROWS, 128), np.float32)
    rows = np.arange(N1 // 2 + 1)
    for column in range(NOFF):
        along_x = d1[:, None] + 20.0 * (column - R)
        along_y = d2[None, :] + 3.0 * (column - R)
        spread = along_x * along_x + along_y * along_y + SOFTEN
        for part, value in enumerate((along_x / spread, along_y / spread)):
            hat = np.fft.fft2(value)[:, : N2 // 2 + 1] * scale
            for half_index, pick in enumerate((rows, (-rows) % N1)):
                place = slice(half_index * ROWS, half_index * ROWS + rows.size)
                spectra[column, part, 0, place, : N2 // 2 + 1] = hat[pick].real
                spectra[column, part, 1, place, : N2 // 2 + 1] = hat[pick].imag
    return fwd_y, fwd_x, inv_x, inv_y, spectra


def exchange_kernel(
    groups, doms,
    pos_any, sl_any, enc_any, g_ref, e_ref,
    pos_ref, sl_ref, enc_ref, block, encs, in_sem, sems,
):
    n = lax.axis_index("bunch")
    me = lax.axis_index("dom")
    loads = [
        pltpu.make_async_copy(src, dst, in_sem.at[k])
        for k, (src, dst) in enumerate(((pos_any, pos_ref), (sl_any, sl_ref), (enc_any, enc_ref)))
    ]
    for load in loads:
        load.start()
    peers = []
    for off in (1, -1, 0):
        for j in range(doms):
            if off == 0 and j == 0:
                continue
            peers.append((off, lax.rem(n + off + groups, groups), lax.rem(me + j, doms)))

    barrier = pltpu.get_barrier_semaphore()
    for _, there, dom in peers:
        pl.semaphore_signal(barrier, inc=1, device_id=(there, dom), device_id_type=MESH)

    for load in loads:
        load.wait()
    centre = 0.5 * (G - 1)
    for beam in range(2):
        gap = sl_ref[beam].astype(F32)
        block[beam * 8 : beam * 8 + 4, :] = (centre + pos_ref[0, beam]) + 4.0 * gap
        block[beam * 8 + 4 : beam * 8 + 8, :] = (centre + pos_ref[1, beam]) + gap
    encs[...] = jnp.zeros_like(encs)
    encs[0:BUN, 0:NOFF] = enc_ref[...]
    pl.semaphore_wait(barrier, len(peers))

    for off in (1, -1):
        pltpu.make_async_remote_copy(
            src_ref=encs,
            dst_ref=e_ref.at[1 - off],
            send_sem=sems.at[0],
            recv_sem=sems.at[1],
            device_id=(lax.rem(n + off + groups, groups), me),
            device_id_type=MESH,
        ).start()
    for off, there, dom in peers:
        pltpu.make_async_remote_copy(
            src_ref=block,
            dst_ref=g_ref.at[(1 - off) * doms + me],
            send_sem=sems.at[2],
            recv_sem=sems.at[3],
            device_id=(there, dom),
            device_id_type=MESH,
        ).start()
    pltpu.make_async_copy(encs, e_ref.at[1], sems.at[1]).start()
    pltpu.make_async_copy(block, g_ref.at[doms + me], sems.at[3]).start()
    for sem, ref in ((3, g_ref), (1, e_ref), (2, g_ref.at[pl.ds(0, len(peers))]), (0, e_ref.at[pl.ds(0, 2)])):
        pltpu.make_async_copy(ref, ref, sems.at[sem]).wait()


def high_low(values):
    high = values.astype(BF)
    return high, (values - high.astype(F32)).astype(BF)


def mm(a, b):
    return jnp.dot(a, b, preferred_element_type=F32)


def live_lists(enc_ref, order, place, pair_c, pair_p, pair_count):
    flags = []
    for beam in range(2):
        for b in range(BUN):
            row = []
            for c in range(NOFF):
                if beam == 0:
                    row.append(enc_ref[1, b, c])
                else:
                    a = b + c + 1
                    row.append(enc_ref[a // BUN, a % BUN, 2 * R - c])
            flags.append(row)
    count = jnp.int32(0)
    for k in range(2 * SRC + 8):
        order[k] = 0
    for source in ALWAYS:
        place[source] = count
        order[count] = source
        count = count + 1
    for source in range(2 * SRC):
        if source in ALWAYS:
            continue
        beam, m = source // SRC, source % SRC
        users = [flags[(1 - beam) * BUN + b][m - b] for b in range(BUN) if 0 <= m - b < NOFF]
        need = users[0]
        for other in users[1:]:
            need = jnp.maximum(need, other)
        order[count] = source
        place[source] = count
        count = count + need
    order[count] = 0
    for target in range(2 * BUN):
        beam, b = target // BUN, target % BUN
        total = jnp.int32(0)
        for c in range(NOFF):
            pair_c[target * 8 + total] = c
            pair_p[target * 8 + total] = place[(1 - beam) * SRC + b + c]
            total = total + flags[target][c]
        pair_count[target] = total
    return count


def solve_kernel(
    doms,
    g_ref, enc_any, fy_any, fx_any, ix_any, iy_any, kv_any,
    f_any, kick_any,
    fy_ref, fx_ref, ix_ref, iy_ref, kv, table_sem,
    q, wx, wy, grids, spec, acc, bh_ref, bl_ref, win, kick_ref,
    enc_ref, order, place, pair_c, pair_p, pair_count, enc_sem, out_sem,
):
    enc_load = pltpu.make_async_copy(enc_any, enc_ref, enc_sem)
    enc_load.start()
    pairs = ((fy_any, fy_ref), (fx_any, fx_ref), (kv_any, kv), (ix_any, ix_ref), (iy_any, iy_ref))
    loads = [pltpu.make_async_copy(src, dst, table_sem.at[k]) for k, (src, dst) in enumerate(pairs)]
    for load in loads:
        load.start()

    where_at = g_ref[...]
    cell = jnp.floor(where_at)
    upper = where_at - cell
    q[0] = cell
    for slot, part in ((1, 1.0 - upper), (3, upper)):
        high = part.astype(BF).astype(F32)
        q[slot] = high
        q[slot + 1] = part - high

    line = lax.broadcasted_iota(jnp.int32, (16, 128), 0).astype(F32)
    lines = [(line + 16.0 * t).astype(BF) for t in range(ROWS // 16)]
    below = [(line + (16.0 * t - 1.0)).astype(BF) for t in range(ROWS // 16)]
    nothing = jnp.zeros((16, 128), BF)

    def weights(source, slot):
        beam = source // SRC
        m = source - beam * SRC
        grp = (m + 1) // BUN
        bunch = (m + 1) % BUN
        for coord, dest in ((0, wx[slot]), (1, wy[slot])):
            row = beam * 8 + coord * 4 + bunch
            for d in range(doms):
                cells, lh, ll, uh, ul = [
                    jnp.broadcast_to(q[j, grp * doms + d, pl.ds(row, 1), :], (16, 128)).astype(BF) for j in range(5)
                ]
                cols = slice(d * 128, (d + 1) * 128)
                for t in range(ROWS // 16):
                    first = lines[t] == cells
                    second = below[t] == cells
                    dest[16 * t : 16 * t + 16, cols] = jnp.where(first, lh, jnp.where(second, uh, nothing))
                    dest[ROWS + 16 * t : ROWS + 16 * t + 16, cols] = jnp.where(
                        first, ll, jnp.where(second, ul, nothing)
                    )

    def deposit(slot):
        both = lax.dot_general(
            wx[slot][...], wy[slot][...], (((1,), (1,)), ((), ())), preferred_element_type=F32
        )
        both = both[:ROWS] + both[ROWS:]
        high, low = high_low(both[:, :ROWS] + both[:, ROWS:])
        grids[slot][...] = jnp.concatenate([high, low, high], axis=1)

    def spectra(k, slots):
        first = mm(jnp.concatenate([grids[slot][...] for slot in slots], axis=0), fy_ref[...])
        for s in range(len(slots)):
            high, low = high_low(first[s * ROWS : (s + 1) * ROWS])
            out = mm(fx_ref[...], jnp.concatenate([high, low, high], axis=0))
            cr, ci = out[:ROWS, :128], out[:ROWS, 128:]
            sr, si = out[ROWS:, :128], out[ROWS:, 128:]
            spec[k + s, 0, :ROWS] = cr + si
            spec[k + s, 0, ROWS:] = cr - si
            spec[k + s, 1, :ROWS] = ci - sr
            spec[k + s, 1, ROWS:] = ci + sr

    for s in range(4):
        weights(ALWAYS[s], s)
    enc_load.wait()
    count = live_lists(enc_ref, order, place, pair_c, pair_p, pair_count)
    for s in range(4):
        deposit(s)
        weights(order[4 + s], s)
    for load in loads[:2]:
        load.wait()

    def four_sources(j, _):
        k = 4 * j
        for half in (0, 2):
            spectra(k - 4 + half, (half, half + 1))
        for s in range(4):
            deposit(s)
            weights(order[k + 4 + s], s)
        return 0

    turns = (count + 1) // 4
    lax.fori_loop(1, turns, four_sources, 0)

    @pl.when(count > 4 * turns)
    def _():
        for half in (0, 2):
            spectra(4 * turns - 4 + half, (half, half + 1))
        for s in range(2):
            deposit(s)
        spectra(4 * turns, (0, 1))

    @pl.when(count <= 4 * turns)
    def _():
        for half in (0, 2):
            spectra(4 * turns - 4 + half, (half, half + 1))

    for load in loads[2:]:
        load.wait()

    me = lax.axis_index("dom")
    index = lax.broadcasted_iota(jnp.int32, (ROWS, 128), 0).astype(F32)

    def multiply(target, _):
        for rows in (slice(0, ROWS), slice(ROWS, 2 * ROWS)):

            def partner(j, sums):
                c = pair_c[target * 8 + j]
                p = pair_p[target * 8 + j]
                re, im = spec[p, 0, rows], spec[p, 1, rows]
                out = []
                for part in range(2):
                    kr, ki = kv[c, part, 0, rows], kv[c, part, 1, rows]
                    out.append(sums[2 * part] + (kr * re - ki * im))
                    out.append(sums[2 * part + 1] + (kr * im + ki * re))
                return tuple(out)

            zero = jnp.zeros((ROWS, 128), F32)
            sums = lax.fori_loop(0, pair_count[target], partner, (zero,) * 4)
            for part in range(2):
                acc[target, part, 0, rows] = sums[2 * part]
                acc[target, part, 1, rows] = sums[2 * part + 1]
        return 0

    lax.fori_loop(0, 2 * BUN, multiply, 0)

    def finish(beam, _):
        for b in range(BUN):
            target = beam * BUN + b
            stacks = []
            for part in range(2):
                rp, rm = acc[target, part, 0, :ROWS], acc[target, part, 0, ROWS:]
                ip, im = acc[target, part, 1, :ROWS], acc[target, part, 1, ROWS:]
                top = jnp.concatenate([rp + rm, ip + im], axis=1)
                low = jnp.concatenate([im - ip, rp - rm], axis=1)
                dh, dl = high_low(jnp.concatenate([top, low], axis=0))
                stacks.append(jnp.concatenate([dh, dl, dh], axis=0))
            first = mm(ix_ref[...], jnp.concatenate(stacks, axis=1))
            for part in range(2):
                rows = slice((2 * b + part) * ROWS, (2 * b + part + 1) * ROWS)
                bh_ref[rows], bl_ref[rows] = high_low(first[:, 256 * part : 256 * part + 256])
        wide = mm(bh_ref[...], iy_ref[...])
        fields = wide[:, :128] + wide[:, 128:] + mm(bl_ref[...], iy_ref[:, :128])
        for b in range(BUN):
            for part in range(2):
                for i in range(SLICES):
                    top = (2 * b + part) * ROWS + 4 * i
                    win[beam, b, i, part] = fields[top : top + G, i : i + G]
        pltpu.make_async_copy(win.at[beam], f_any.at[beam], out_sem.at[beam]).start()
        for b in range(BUN):
            x = jnp.broadcast_to(g_ref[doms + me, pl.ds(beam * 8 + b, 1), :], (ROWS, 128))
            y = jnp.broadcast_to(g_ref[doms + me, pl.ds(beam * 8 + 4 + b, 1), :], (ROWS, 128))
            weight_x = jnp.maximum(0.0, 1.0 - jnp.abs(x - index))
            yh, yl = high_low(jnp.maximum(0.0, 1.0 - jnp.abs(y - index)))
            fh, fl = high_low(fields[2 * b * ROWS : 2 * (b + 1) * ROWS, :ROWS])
            both = mm(jnp.concatenate([fh, fl], axis=0), jnp.concatenate([yh, yl], axis=1))
            sampled = both[: 2 * ROWS, :128] + both[2 * ROWS :, :128] + both[: 2 * ROWS, 128:]
            for part in range(2):
                kick_ref[part, beam, b : b + 1, :] = jnp.sum(
                    weight_x * sampled[part * ROWS : (part + 1) * ROWS], axis=0, keepdims=True
                )
        return 0

    lax.fori_loop(0, 2, finish, 0)
    kicks = pltpu.make_async_copy(kick_ref, kick_any, enc_sem)
    kicks.start()
    for beam in range(2):
        pltpu.make_async_copy(win.at[beam], f_any.at[beam], out_sem.at[beam]).wait()
    kicks.wait()


def solve(gathered, enc):
    doms, particles = gathered.shape[0] // 3, gathered.shape[2]
    vmem = pl.BlockSpec(memory_space=pltpu.VMEM)
    anywhere = pl.BlockSpec(memory_space=pl.ANY)
    consts = [jnp.asarray(t) for t in tables(CHARGE / (particles * doms))]
    weight = pltpu.VMEM((2 * ROWS, doms * particles), BF)
    return pl.pallas_call(
        functools.partial(solve_kernel, doms),
        out_shape=(
            jax.ShapeDtypeStruct((2, BUN, SLICES, 2, G, G), F32),
            jax.ShapeDtypeStruct((2, 2, BUN, particles), F32),
        ),
        in_specs=[vmem] + [anywhere] * (1 + len(consts)),
        out_specs=(anywhere, anywhere),
        scratch_shapes=[pltpu.VMEM(t.shape, t.dtype) for t in consts] + [
            pltpu.SemaphoreType.DMA((len(consts),)),
            pltpu.VMEM((5, 3 * doms, 16, particles), F32),
            [weight] * 4,
            [weight] * 4,
            [pltpu.VMEM((ROWS, 3 * ROWS), BF)] * 4,
            pltpu.VMEM((2 * SRC + 4, 2, 2 * ROWS, 128), F32),
            pltpu.VMEM((2 * BUN, 2, 2, 2 * ROWS, 128), F32),
            pltpu.VMEM((BUN * 2 * ROWS, 256), BF),
            pltpu.VMEM((BUN * 2 * ROWS, 256), BF),
            pltpu.VMEM((2, BUN, SLICES, 2, G, G), F32),
            pltpu.VMEM((2, 2, BUN, particles), F32),
            pltpu.SMEM((3, 8, 128), jnp.int32),
            pltpu.SMEM((2 * SRC + 8,), jnp.int32),
            pltpu.SMEM((2 * SRC,), jnp.int32),
            pltpu.SMEM((2 * BUN * 8,), jnp.int32),
            pltpu.SMEM((2 * BUN * 8,), jnp.int32),
            pltpu.SMEM((2 * BUN,), jnp.int32),
            pltpu.SemaphoreType.DMA,
            pltpu.SemaphoreType.DMA((2,)),
        ],
        compiler_params=pltpu.CompilerParams(vmem_limit_bytes=24 * 1024 * 1024),
        name="solve",
    )(gathered, enc, *[pltpu.with_memory_space_constraint(t, pltpu.HBM) for t in consts])


def on_device(positions, slice_index, encounters):
    groups, doms = lax.axis_size("bunch"), lax.axis_size("dom")
    particles = positions.shape[3]
    anywhere = pl.BlockSpec(memory_space=pl.ANY)
    gathered, enc = pl.pallas_call(
        functools.partial(exchange_kernel, groups, doms),
        out_shape=(
            jax.ShapeDtypeStruct((3 * doms, 16, particles), F32),
            jax.ShapeDtypeStruct((3, 8, 128), jnp.int32),
        ),
        in_specs=[anywhere] * 3,
        out_specs=(anywhere, anywhere),
        scratch_shapes=[
            pltpu.VMEM(positions.shape, F32),
            pltpu.VMEM(slice_index.shape, jnp.int32),
            pltpu.VMEM(encounters.shape, jnp.int32),
            pltpu.VMEM((16, particles), F32),
            pltpu.VMEM((8, 128), jnp.int32),
            pltpu.SemaphoreType.DMA((3,)),
            pltpu.SemaphoreType.DMA((4,)),
        ],
        compiler_params=pltpu.CompilerParams(
            collective_id=0, has_side_effects=True, vmem_limit_bytes=1024 * 1024
        ),
        name="exchange",
    )(*[pltpu.with_memory_space_constraint(v, pltpu.HBM) for v in (positions, slice_index, encounters)])
    return solve(gathered, enc)


def solution(mesh):
    placed = (P(None, None, "bunch", "dom"), P(None, "bunch", "dom"), P("bunch", None))
    return jax.shard_map(
        on_device,
        mesh=mesh,
        in_specs=placed,
        out_specs=(P(None, "bunch", None, None, None, None), P(None, None, "bunch", "dom")),
        check_vma=False,
    )
```

```python
import functools

import jax
import jax.numpy as jnp
import ml_dtypes
import numpy as np
from jax import lax
from jax.experimental import pallas as pl
from jax.experimental.pallas import tpu as pltpu
from jax.sharding import PartitionSpec as P

G = 64
SLICES = 4
R = 3
NOFF = 7
CHARGE = 8.0
SOFTEN = 1.0

BUN = 4
SRC = BUN + 2 * R
ALWAYS = (SRC, 2 * SRC - 1, R - 1, R + BUN)
N1 = 152
N2 = 134
ROWS = 80
MESH = pl.DeviceIdType.MESH
BF = jnp.bfloat16
F32 = jnp.float32


def split_table(values):
    high = values.astype(ml_dtypes.bfloat16)
    low = (values - high.astype(np.float64)).astype(ml_dtypes.bfloat16)
    return high, low


@functools.lru_cache(maxsize=None)
def tables(scale):
    line = np.arange(ROWS)
    kx = np.arange(ROWS)
    live_kx = (kx <= N1 // 2).astype(np.float64)
    ky = np.arange(128)
    live_ky = (ky <= N2 // 2).astype(np.float64)

    phase_y = 2.0 * np.pi * (line[:, None] * ky[None, :] % N2) / N2
    along = np.concatenate([np.cos(phase_y) * live_ky, -np.sin(phase_y) * live_ky], axis=1)
    high, low = split_table(along)
    fwd_y = np.concatenate([high, high, low], axis=0)

    phase_x = 2.0 * np.pi * (kx[:, None] * line[None, :] % N1) / N1
    cos_x = np.cos(phase_x) * live_kx[:, None]
    sin_x = np.sin(phase_x) * live_kx[:, None]
    high, low = split_table(np.concatenate([cos_x, sin_x], axis=0))
    fwd_x = np.concatenate([high, high, low], axis=1)

    half = np.where((kx == 0) | (kx == N1 // 2), 0.5, 1.0) / (N1 * N2)
    high, low = split_table(np.concatenate([(cos_x * half[:, None]).T, (sin_x * half[:, None]).T], axis=1))
    inv_x = np.concatenate([high, high, low], axis=1)

    twice = np.where((ky == 0) | (ky == N2 // 2), 1.0, 2.0) * live_ky
    cell = np.arange(128)
    live_cell = (cell < G + SLICES - 1).astype(np.float64)
    phase = 2.0 * np.pi * (ky[:, None] * cell[None, :] % N2) / N2
    back = np.concatenate([np.cos(phase) * twice[:, None], -np.sin(phase) * twice[:, None]], axis=0)
    inv_y = np.concatenate(split_table(back * live_cell[None, :]), axis=1)

    d1 = np.arange(N1)
    d1 = np.where(d1 < N1 // 2, d1, d1 - N1).astype(np.float64)
    d2 = np.arange(N2)
    d2 = np.where(d2 < N2 // 2, d2, d2 - N2).astype(np.float64)
    spectra = np.zeros((NOFF, 2, 2, 2 * ROWS, 128), np.float32)
    rows = np.arange(N1 // 2 + 1)
    for column in range(NOFF):
        along_x = d1[:, None] + 20.0 * (column - R)
        along_y = d2[None, :] + 3.0 * (column - R)
        spread = along_x * along_x + along_y * along_y + SOFTEN
        for part, value in enumerate((along_x / spread, along_y / spread)):
            hat = np.fft.fft2(value)[:, : N2 // 2 + 1] * scale
            for half_index, pick in enumerate((rows, (-rows) % N1)):
                place = slice(half_index * ROWS, half_index * ROWS + rows.size)
                spectra[column, part, 0, place, : N2 // 2 + 1] = hat[pick].real
                spectra[column, part, 1, place, : N2 // 2 + 1] = hat[pick].imag
    return fwd_y, fwd_x, inv_x, inv_y, spectra


def exchange_kernel(
    groups, doms,
    pos_any, sl_any, enc_any, g_ref, e_ref,
    pos_ref, sl_ref, enc_ref, block, encs, in_sem, sems,
):
    n = lax.axis_index("bunch")
    me = lax.axis_index("dom")
    loads = [
        pltpu.make_async_copy(src, dst, in_sem.at[k])
        for k, (src, dst) in enumerate(((pos_any, pos_ref), (sl_any, sl_ref), (enc_any, enc_ref)))
    ]
    for load in loads:
        load.start()
    peers = []
    for off in (1, -1, 0):
        for j in range(doms):
            if off == 0 and j == 0:
                continue
            peers.append((off, lax.rem(n + off + groups, groups), lax.rem(me + j, doms)))

    barrier = pltpu.get_barrier_semaphore()
    for _, there, dom in peers:
        pl.semaphore_signal(barrier, inc=1, device_id=(there, dom), device_id_type=MESH)

    for load in loads:
        load.wait()
    centre = 0.5 * (G - 1)
    for beam in range(2):
        gap = sl_ref[beam].astype(F32)
        block[beam * 8 : beam * 8 + 4, :] = (centre + pos_ref[0, beam]) + 4.0 * gap
        block[beam * 8 + 4 : beam * 8 + 8, :] = (centre + pos_ref[1, beam]) + gap
    encs[...] = jnp.zeros_like(encs)
    encs[0:BUN, 0:NOFF] = enc_ref[...]
    pl.semaphore_wait(barrier, len(peers))

    for off in (1, -1):
        pltpu.make_async_remote_copy(
            src_ref=encs,
            dst_ref=e_ref.at[1 - off],
            send_sem=sems.at[0],
            recv_sem=sems.at[1],
            device_id=(lax.rem(n + off + groups, groups), me),
            device_id_type=MESH,
        ).start()
    for off, there, dom in peers:
        pltpu.make_async_remote_copy(
            src_ref=block,
            dst_ref=g_ref.at[(1 - off) * doms + me],
            send_sem=sems.at[2],
            recv_sem=sems.at[3],
            device_id=(there, dom),
            device_id_type=MESH,
        ).start()
    pltpu.make_async_copy(encs, e_ref.at[1], sems.at[1]).start()
    pltpu.make_async_copy(block, g_ref.at[doms + me], sems.at[3]).start()
    for sem, ref in ((3, g_ref), (1, e_ref), (2, g_ref.at[pl.ds(0, len(peers))]), (0, e_ref.at[pl.ds(0, 2)])):
        pltpu.make_async_copy(ref, ref, sems.at[sem]).wait()


def high_low(values):
    high = values.astype(BF)
    return high, (values - high.astype(F32)).astype(BF)


def mm(a, b):
    return jnp.dot(a, b, preferred_element_type=F32)


def live_lists(enc_ref, order, place, pair_c, pair_p, pair_count):
    flags = []
    for beam in range(2):
        for b in range(BUN):
            row = []
            for c in range(NOFF):
                if beam == 0:
                    row.append(enc_ref[1, b, c])
                else:
                    a = b + c + 1
                    row.append(enc_ref[a // BUN, a % BUN, 2 * R - c])
            flags.append(row)
    count = jnp.int32(0)
    for k in range(2 * SRC + 8):
        order[k] = 0
    for source in ALWAYS:
        place[source] = count
        order[count] = source
        count = count + 1
    for source in range(2 * SRC):
        if source in ALWAYS:
            continue
        beam, m = source // SRC, source % SRC
        users = [flags[(1 - beam) * BUN + b][m - b] for b in range(BUN) if 0 <= m - b < NOFF]
        need = users[0]
        for other in users[1:]:
            need = jnp.maximum(need, other)
        order[count] = source
        place[source] = count
        count = count + need
    order[count] = 0
    for target in range(2 * BUN):
        beam, b = target // BUN, target % BUN
        total = jnp.int32(0)
        for c in range(NOFF):
            pair_c[target * 8 + total] = c
            pair_p[target * 8 + total] = place[(1 - beam) * SRC + b + c]
            total = total + flags[target][c]
        pair_count[target] = total
    return count


def solve_kernel(
    doms,
    g_ref, enc_any, fy_any, fx_any, ix_any, iy_any, kv_any,
    f_any, kick_any,
    fy_ref, fx_ref, ix_ref, iy_ref, kv, table_sem,
    wx, wy, grids, spec, acc, bh_ref, bl_ref, win, kick_ref,
    enc_ref, order, place, pair_c, pair_p, pair_count, enc_sem, out_sem,
):
    enc_load = pltpu.make_async_copy(enc_any, enc_ref, enc_sem)
    enc_load.start()
    pairs = ((fy_any, fy_ref), (fx_any, fx_ref), (kv_any, kv), (ix_any, ix_ref), (iy_any, iy_ref))
    loads = [pltpu.make_async_copy(src, dst, table_sem.at[k]) for k, (src, dst) in enumerate(pairs)]
    for load in loads:
        load.start()

    line = lax.broadcasted_iota(jnp.int32, (16, 128), 0).astype(F32)
    lines = [(line + 16.0 * t).astype(BF) for t in range(ROWS // 16)]
    below = [(line + (16.0 * t - 1.0)).astype(BF) for t in range(ROWS // 16)]
    nothing = jnp.zeros((16, 128), BF)

    def weights(source, slot):
        beam = source // SRC
        m = source - beam * SRC
        grp = (m + 1) // BUN
        bunch = (m + 1) % BUN
        for coord, dest in ((0, wx[slot]), (1, wy[slot])):
            row = beam * 8 + coord * 4 + bunch
            for d in range(doms):
                at = jnp.broadcast_to(g_ref[grp * doms + d, pl.ds(row, 1), :], (8, 128))
                cell = jnp.floor(at)
                upper = at - cell
                lower = 1.0 - upper
                values = [cell, lower, lower - lower.astype(BF).astype(F32), upper, upper - upper.astype(BF).astype(F32)]
                cells, lh, ll, uh, ul = [jnp.concatenate([v, v], axis=0).astype(BF) for v in values]
                cols = slice(d * 128, (d + 1) * 128)
                for t in range(ROWS // 16):
                    first = lines[t] == cells
                    second = below[t] == cells
                    dest[16 * t : 16 * t + 16, cols] = jnp.where(first, lh, jnp.where(second, uh, nothing))
                    dest[ROWS + 16 * t : ROWS + 16 * t + 16, cols] = jnp.where(
                        first, ll, jnp.where(second, ul, nothing)
                    )

    def deposit(slot):
        both = lax.dot_general(
            wx[slot][...], wy[slot][...], (((1,), (1,)), ((), ())), preferred_element_type=F32
        )
        both = both[:ROWS] + both[ROWS:]
        high, low = high_low(both[:, :ROWS] + both[:, ROWS:])
        grids[slot][...] = jnp.concatenate([high, low, high], axis=1)

    def along_y(slots):
        return mm(jnp.concatenate([grids[slot][...] for slot in slots], axis=0), fy_ref[...])

    def along_x(k, first):
        outs = []
        for s in range(first.shape[0] // ROWS):
            high, low = high_low(first[s * ROWS : (s + 1) * ROWS])
            outs.append(mm(fx_ref[...], jnp.concatenate([high, low, high], axis=0)))
        for s, out in enumerate(outs):
            cr, ci = out[:ROWS, :128], out[:ROWS, 128:]
            sr, si = out[ROWS:, :128], out[ROWS:, 128:]
            spec[k + s, 0, :ROWS] = cr + si
            spec[k + s, 0, ROWS:] = cr - si
            spec[k + s, 1, :ROWS] = ci - sr
            spec[k + s, 1, ROWS:] = ci + sr

    for s in range(4):
        weights(ALWAYS[s], s)
    enc_load.wait()
    count = live_lists(enc_ref, order, place, pair_c, pair_p, pair_count)
    for s in range(4):
        deposit(s)
        weights(order[4 + s], s)
    for load in loads[:2]:
        load.wait()

    def four_sources(j, _):
        k = 4 * j
        first, second = along_y((0, 1)), along_y((2, 3))
        for s in range(2):
            deposit(s)
            weights(order[k + 4 + s], s)
        along_x(k - 4, first)
        for s in range(2, 4):
            deposit(s)
            weights(order[k + 4 + s], s)
        along_x(k - 2, second)
        return 0

    turns = (count + 1) // 4
    lax.fori_loop(1, turns, four_sources, 0)

    @pl.when(count > 4 * turns)
    def _():
        first, second = along_y((0, 1)), along_y((2, 3))
        for s in range(2):
            deposit(s)
        along_x(4 * turns - 4, first)
        third = along_y((0, 1))
        along_x(4 * turns - 2, second)
        along_x(4 * turns, third)

    @pl.when(count <= 4 * turns)
    def _():
        first, second = along_y((0, 1)), along_y((2, 3))
        along_x(4 * turns - 4, first)
        along_x(4 * turns - 2, second)

    for load in loads[2:]:
        load.wait()

    me = lax.axis_index("dom")
    index = lax.broadcasted_iota(jnp.int32, (ROWS, 128), 0).astype(F32)

    def multiply(target, _):
        def partner(j, add):
            c = pair_c[target * 8 + j]
            p = pair_p[target * 8 + j]
            for t in range(2 * ROWS // 16):
                rows = slice(16 * t, 16 * t + 16)
                re = spec[p, 0, rows]
                im = spec[p, 1, rows]
                for part in range(2):
                    kr = kv[c, part, 0, rows]
                    ki = kv[c, part, 1, rows]
                    real = kr * re - ki * im
                    imag = kr * im + ki * re
                    if add:
                        real = acc[target, part, 0, rows] + real
                        imag = acc[target, part, 1, rows] + imag
                    acc[target, part, 0, rows] = real
                    acc[target, part, 1, rows] = imag

        def later(j, _):
            partner(j, True)
            return 0

        @pl.when(pair_count[target] == 0)
        def _():
            acc[target] = jnp.zeros_like(acc[target])

        @pl.when(pair_count[target] > 0)
        def _():
            partner(0, False)
            lax.fori_loop(1, pair_count[target], later, 0)

        return 0

    lax.fori_loop(0, 2 * BUN, multiply, 0)

    def finish(beam, _):
        firsts = []
        for b in range(BUN):
            target = beam * BUN + b
            stacks = []
            for part in range(2):
                rp, rm = acc[target, part, 0, :ROWS], acc[target, part, 0, ROWS:]
                ip, im = acc[target, part, 1, :ROWS], acc[target, part, 1, ROWS:]
                top = jnp.concatenate([rp + rm, ip + im], axis=1)
                low = jnp.concatenate([im - ip, rp - rm], axis=1)
                dh, dl = high_low(jnp.concatenate([top, low], axis=0))
                stacks.append(jnp.concatenate([dh, dl, dh], axis=0))
            firsts.append(mm(ix_ref[...], jnp.concatenate(stacks, axis=1)))
        for b, first in enumerate(firsts):
            for part in range(2):
                rows = slice((2 * b + part) * ROWS, (2 * b + part + 1) * ROWS)
                bh_ref[rows], bl_ref[rows] = high_low(first[:, 256 * part : 256 * part + 256])
        wide = mm(bh_ref[...], iy_ref[...])
        fields = wide[:, :128] + wide[:, 128:] + mm(bl_ref[...], iy_ref[:, :128])
        for b in range(BUN):
            for part in range(2):
                for i in range(SLICES):
                    top = (2 * b + part) * ROWS + 4 * i
                    win[beam, b, i, part] = fields[top : top + G, i : i + G]
            pltpu.make_async_copy(win.at[beam, b], f_any.at[beam, b], out_sem.at[beam]).start()
        products = []
        for b in range(BUN):
            y = jnp.broadcast_to(g_ref[doms + me, pl.ds(beam * 8 + 4 + b, 1), :], (ROWS, 128))
            yh, yl = high_low(jnp.maximum(0.0, 1.0 - jnp.abs(y - index)))
            fh, fl = high_low(fields[2 * b * ROWS : 2 * (b + 1) * ROWS, :ROWS])
            products.append(mm(jnp.concatenate([fh, fl], axis=0), jnp.concatenate([yh, yl], axis=1)))
        for b, both in enumerate(products):
            x = jnp.broadcast_to(g_ref[doms + me, pl.ds(beam * 8 + b, 1), :], (ROWS, 128))
            weight_x = jnp.maximum(0.0, 1.0 - jnp.abs(x - index))
            sampled = both[: 2 * ROWS, :128] + both[2 * ROWS :, :128] + both[: 2 * ROWS, 128:]
            for part in range(2):
                kick_ref[part, beam, b : b + 1, :] = jnp.sum(
                    weight_x * sampled[part * ROWS : (part + 1) * ROWS], axis=0, keepdims=True
                )
        return 0

    lax.fori_loop(0, 2, finish, 0)
    kicks = pltpu.make_async_copy(kick_ref, kick_any, enc_sem)
    kicks.start()
    for beam in range(2):
        pltpu.make_async_copy(win.at[beam], f_any.at[beam], out_sem.at[beam]).wait()
    kicks.wait()


def solve(gathered, enc):
    doms, particles = gathered.shape[0] // 3, gathered.shape[2]
    vmem = pl.BlockSpec(memory_space=pltpu.VMEM)
    anywhere = pl.BlockSpec(memory_space=pl.ANY)
    consts = [jnp.asarray(t) for t in tables(CHARGE / (particles * doms))]
    weight = pltpu.VMEM((2 * ROWS, doms * particles), BF)
    return pl.pallas_call(
        functools.partial(solve_kernel, doms),
        out_shape=(
            jax.ShapeDtypeStruct((2, BUN, SLICES, 2, G, G), F32),
            jax.ShapeDtypeStruct((2, 2, BUN, particles), F32),
        ),
        in_specs=[vmem] + [anywhere] * (1 + len(consts)),
        out_specs=(anywhere, anywhere),
        scratch_shapes=[pltpu.VMEM(t.shape, t.dtype) for t in consts] + [
            pltpu.SemaphoreType.DMA((len(consts),)),
            [weight] * 4,
            [weight] * 4,
            [pltpu.VMEM((ROWS, 3 * ROWS), BF)] * 4,
            pltpu.VMEM((2 * SRC + 4, 2, 2 * ROWS, 128), F32),
            pltpu.VMEM((2 * BUN, 2, 2, 2 * ROWS, 128), F32),
            pltpu.VMEM((BUN * 2 * ROWS, 256), BF),
            pltpu.VMEM((BUN * 2 * ROWS, 256), BF),
            pltpu.VMEM((2, BUN, SLICES, 2, G, G), F32),
            pltpu.VMEM((2, 2, BUN, particles), F32),
            pltpu.SMEM((3, 8, 128), jnp.int32),
            pltpu.SMEM((2 * SRC + 8,), jnp.int32),
            pltpu.SMEM((2 * SRC,), jnp.int32),
            pltpu.SMEM((2 * BUN * 8,), jnp.int32),
            pltpu.SMEM((2 * BUN * 8,), jnp.int32),
            pltpu.SMEM((2 * BUN,), jnp.int32),
            pltpu.SemaphoreType.DMA,
            pltpu.SemaphoreType.DMA((2,)),
        ],
        compiler_params=pltpu.CompilerParams(vmem_limit_bytes=24 * 1024 * 1024),
        name="solve",
    )(gathered, enc, *[pltpu.with_memory_space_constraint(t, pltpu.HBM) for t in consts])


def on_device(positions, slice_index, encounters):
    groups, doms = lax.axis_size("bunch"), lax.axis_size("dom")
    particles = positions.shape[3]
    anywhere = pl.BlockSpec(memory_space=pl.ANY)
    gathered, enc = pl.pallas_call(
        functools.partial(exchange_kernel, groups, doms),
        out_shape=(
            jax.ShapeDtypeStruct((3 * doms, 16, particles), F32),
            jax.ShapeDtypeStruct((3, 8, 128), jnp.int32),
        ),
        in_specs=[anywhere] * 3,
        out_specs=(anywhere, anywhere),
        scratch_shapes=[
            pltpu.VMEM(positions.shape, F32),
            pltpu.VMEM(slice_index.shape, jnp.int32),
            pltpu.VMEM(encounters.shape, jnp.int32),
            pltpu.VMEM((16, particles), F32),
            pltpu.VMEM((8, 128), jnp.int32),
            pltpu.SemaphoreType.DMA((3,)),
            pltpu.SemaphoreType.DMA((4,)),
        ],
        compiler_params=pltpu.CompilerParams(
            collective_id=0, has_side_effects=True, vmem_limit_bytes=1024 * 1024
        ),
        name="exchange",
    )(*[pltpu.with_memory_space_constraint(v, pltpu.HBM) for v in (positions, slice_index, encounters)])
    return solve(gathered, enc)


def solution(mesh):
    placed = (P(None, None, "bunch", "dom"), P(None, "bunch", "dom"), P("bunch", None))
    return jax.shard_map(
        on_device,
        mesh=mesh,
        in_specs=placed,
        out_specs=(P(None, "bunch", None, None, None, None), P(None, None, "bunch", "dom")),
        check_vma=False,
    )
```

```python
import functools

import jax
import jax.numpy as jnp
import ml_dtypes
import numpy as np
from jax import lax
from jax.experimental import pallas as pl
from jax.experimental.pallas import tpu as pltpu
from jax.sharding import PartitionSpec as P

G = 64
SLICES = 4
R = 3
NOFF = 7
CHARGE = 8.0
SOFTEN = 1.0

BUN = 4
SRC = BUN + 2 * R
ALWAYS = (SRC, 2 * SRC - 1, R - 1, R + BUN)
N1 = 152
N2 = 134
ROWS = 80
MESH = pl.DeviceIdType.MESH
BF = jnp.bfloat16
F32 = jnp.float32


def split_table(values):
    high = values.astype(ml_dtypes.bfloat16)
    low = (values - high.astype(np.float64)).astype(ml_dtypes.bfloat16)
    return high, low


@functools.lru_cache(maxsize=None)
def tables(scale):
    line = np.arange(ROWS)
    kx = np.arange(ROWS)
    live_kx = (kx <= N1 // 2).astype(np.float64)
    ky = np.arange(128)
    live_ky = (ky <= N2 // 2).astype(np.float64)

    phase_y = 2.0 * np.pi * (line[:, None] * ky[None, :] % N2) / N2
    along = np.concatenate([np.cos(phase_y) * live_ky, -np.sin(phase_y) * live_ky], axis=1)
    high, low = split_table(along)
    fwd_y = np.concatenate([high, high, low], axis=0)

    phase_x = 2.0 * np.pi * (kx[:, None] * line[None, :] % N1) / N1
    cos_x = np.cos(phase_x) * live_kx[:, None]
    sin_x = np.sin(phase_x) * live_kx[:, None]
    high, low = split_table(np.concatenate([cos_x, sin_x], axis=0))
    fwd_x = np.concatenate([high, high, low], axis=1)

    half = np.where((kx == 0) | (kx == N1 // 2), 0.5, 1.0) / (N1 * N2)
    high, low = split_table(np.concatenate([(cos_x * half[:, None]).T, (sin_x * half[:, None]).T], axis=1))
    inv_x = np.concatenate([high, high, low], axis=1)

    twice = np.where((ky == 0) | (ky == N2 // 2), 1.0, 2.0) * live_ky
    cell = np.arange(128)
    live_cell = (cell < G + SLICES - 1).astype(np.float64)
    phase = 2.0 * np.pi * (ky[:, None] * cell[None, :] % N2) / N2
    back = np.concatenate([np.cos(phase) * twice[:, None], -np.sin(phase) * twice[:, None]], axis=0)
    inv_y = np.concatenate(split_table(back * live_cell[None, :]), axis=1)

    d1 = np.arange(N1)
    d1 = np.where(d1 < N1 // 2, d1, d1 - N1).astype(np.float64)
    d2 = np.arange(N2)
    d2 = np.where(d2 < N2 // 2, d2, d2 - N2).astype(np.float64)
    spectra = np.zeros((NOFF, 2, 2, 2 * ROWS, 128), np.float32)
    rows = np.arange(N1 // 2 + 1)
    for column in range(NOFF):
        along_x = d1[:, None] + 20.0 * (column - R)
        along_y = d2[None, :] + 3.0 * (column - R)
        spread = along_x * along_x + along_y * along_y + SOFTEN
        for part, value in enumerate((along_x / spread, along_y / spread)):
            hat = np.fft.fft2(value)[:, : N2 // 2 + 1] * scale
            for half_index, pick in enumerate((rows, (-rows) % N1)):
                place = slice(half_index * ROWS, half_index * ROWS + rows.size)
                spectra[column, part, 0, place, : N2 // 2 + 1] = hat[pick].real
                spectra[column, part, 1, place, : N2 // 2 + 1] = hat[pick].imag
    return fwd_y, fwd_x, inv_x, inv_y, spectra


def exchange_kernel(
    groups, doms,
    pos_any, sl_any, enc_any, g_ref, e_ref,
    pos_ref, sl_ref, enc_ref, block, encs, in_sem, sems,
):
    n = lax.axis_index("bunch")
    me = lax.axis_index("dom")
    loads = [
        pltpu.make_async_copy(src, dst, in_sem.at[k])
        for k, (src, dst) in enumerate(((pos_any, pos_ref), (sl_any, sl_ref), (enc_any, enc_ref)))
    ]
    for load in loads:
        load.start()
    peers = []
    for off in (1, -1, 0):
        for j in range(doms):
            if off == 0 and j == 0:
                continue
            peers.append((off, lax.rem(n + off + groups, groups), lax.rem(me + j, doms)))

    barrier = pltpu.get_barrier_semaphore()
    for _, there, dom in peers:
        pl.semaphore_signal(barrier, inc=1, device_id=(there, dom), device_id_type=MESH)

    for load in loads:
        load.wait()
    centre = 0.5 * (G - 1)
    for beam in range(2):
        gap = sl_ref[beam].astype(F32)
        block[beam * 8 : beam * 8 + 4, :] = (centre + pos_ref[0, beam]) + 4.0 * gap
        block[beam * 8 + 4 : beam * 8 + 8, :] = (centre + pos_ref[1, beam]) + gap
    encs[...] = jnp.zeros_like(encs)
    encs[0:BUN, 0:NOFF] = enc_ref[...]
    pl.semaphore_wait(barrier, len(peers))

    for off in (1, -1):
        pltpu.make_async_remote_copy(
            src_ref=encs,
            dst_ref=e_ref.at[1 - off],
            send_sem=sems.at[0],
            recv_sem=sems.at[1],
            device_id=(lax.rem(n + off + groups, groups), me),
            device_id_type=MESH,
        ).start()
    for off, there, dom in peers:
        pltpu.make_async_remote_copy(
            src_ref=block,
            dst_ref=g_ref.at[(1 - off) * doms + me],
            send_sem=sems.at[2],
            recv_sem=sems.at[3],
            device_id=(there, dom),
            device_id_type=MESH,
        ).start()
    pltpu.make_async_copy(encs, e_ref.at[1], sems.at[1]).start()
    pltpu.make_async_copy(block, g_ref.at[doms + me], sems.at[3]).start()
    for sem, ref in ((3, g_ref), (1, e_ref), (2, g_ref.at[pl.ds(0, len(peers))]), (0, e_ref.at[pl.ds(0, 2)])):
        pltpu.make_async_copy(ref, ref, sems.at[sem]).wait()


def high_low(values):
    high = values.astype(BF)
    return high, (values - high.astype(F32)).astype(BF)


def mm(a, b):
    return jnp.dot(a, b, preferred_element_type=F32)


def live_lists(enc_ref, order, place, pair_c, pair_p, pair_count):
    flags = []
    for beam in range(2):
        for b in range(BUN):
            row = []
            for c in range(NOFF):
                if beam == 0:
                    row.append(enc_ref[1, b, c])
                else:
                    a = b + c + 1
                    row.append(enc_ref[a // BUN, a % BUN, 2 * R - c])
            flags.append(row)
    count = jnp.int32(0)
    for k in range(2 * SRC + 8):
        order[k] = 0
    for source in ALWAYS:
        place[source] = count
        order[count] = source
        count = count + 1
    for source in range(2 * SRC):
        if source in ALWAYS:
            continue
        beam, m = source // SRC, source % SRC
        users = [flags[(1 - beam) * BUN + b][m - b] for b in range(BUN) if 0 <= m - b < NOFF]
        need = users[0]
        for other in users[1:]:
            need = jnp.maximum(need, other)
        order[count] = source
        place[source] = count
        count = count + need
    order[count] = 0
    for target in range(2 * BUN):
        beam, b = target // BUN, target % BUN
        total = jnp.int32(0)
        for c in range(NOFF):
            pair_c[target * 8 + total] = c
            pair_p[target * 8 + total] = place[(1 - beam) * SRC + b + c]
            total = total + flags[target][c]
        pair_count[target] = total
    return count


def solve_kernel(
    doms,
    g_ref, enc_any, fy_any, fx_any, ix_any, iy_any, kv_any,
    f_any, kick_any,
    fy_ref, fx_ref, ix_ref, iy_ref, kv, table_sem,
    wx, wy, grids, spec, acc, bh_ref, bl_ref, win, kick_ref,
    enc_ref, order, place, pair_c, pair_p, pair_count, enc_sem, out_sem,
):
    enc_load = pltpu.make_async_copy(enc_any, enc_ref, enc_sem)
    enc_load.start()
    pairs = ((fy_any, fy_ref), (fx_any, fx_ref), (kv_any, kv), (ix_any, ix_ref), (iy_any, iy_ref))
    loads = [pltpu.make_async_copy(src, dst, table_sem.at[k]) for k, (src, dst) in enumerate(pairs)]
    for load in loads:
        load.start()

    line = lax.broadcasted_iota(jnp.int32, (16, 128), 0).astype(F32)
    lines = [(line + 16.0 * t).astype(BF) for t in range(ROWS // 16)]
    below = [(line + (16.0 * t - 1.0)).astype(BF) for t in range(ROWS // 16)]
    nothing = jnp.zeros((16, 128), BF)

    def weights(source, slot):
        beam = source // SRC
        m = source - beam * SRC
        grp = (m + 1) // BUN
        bunch = (m + 1) % BUN
        for coord, dest in ((0, wx[slot]), (1, wy[slot])):
            row = beam * 8 + coord * 4 + bunch
            for d in range(doms):
                at = jnp.broadcast_to(g_ref[grp * doms + d, pl.ds(row, 1), :], (8, 128))
                cell = jnp.floor(at)
                upper = at - cell
                lower = 1.0 - upper
                values = [cell, lower, lower - lower.astype(BF).astype(F32), upper, upper - upper.astype(BF).astype(F32)]
                cells, lh, ll, uh, ul = [jnp.concatenate([v, v], axis=0).astype(BF) for v in values]
                cols = slice(d * 128, (d + 1) * 128)
                for t in range(ROWS // 16):
                    first = lines[t] == cells
                    second = below[t] == cells
                    dest[16 * t : 16 * t + 16, cols] = jnp.where(first, lh, jnp.where(second, uh, nothing))
                    dest[ROWS + 16 * t : ROWS + 16 * t + 16, cols] = jnp.where(
                        first, ll, jnp.where(second, ul, nothing)
                    )

    def deposit(slot):
        both = lax.dot_general(
            wx[slot][...], wy[slot][...], (((1,), (1,)), ((), ())), preferred_element_type=F32
        )
        both = both[:ROWS] + both[ROWS:]
        high, low = high_low(both[:, :ROWS] + both[:, ROWS:])
        grids[slot][...] = jnp.concatenate([high, low, high], axis=1)

    def along_y(slots):
        return mm(jnp.concatenate([grids[slot][...] for slot in slots], axis=0), fy_ref[...])

    def along_x(k, first):
        outs = []
        for s in range(first.shape[0] // ROWS):
            high, low = high_low(first[s * ROWS : (s + 1) * ROWS])
            outs.append(mm(fx_ref[...], jnp.concatenate([high, low, high], axis=0)))
        for s, out in enumerate(outs):
            cr, ci = out[:ROWS, :128], out[:ROWS, 128:]
            sr, si = out[ROWS:, :128], out[ROWS:, 128:]
            spec[k + s, 0, :ROWS] = cr + si
            spec[k + s, 0, ROWS:] = cr - si
            spec[k + s, 1, :ROWS] = ci - sr
            spec[k + s, 1, ROWS:] = ci + sr

    for s in range(4):
        weights(ALWAYS[s], s)
    enc_load.wait()
    count = live_lists(enc_ref, order, place, pair_c, pair_p, pair_count)
    deposit(0)
    for s in range(1, 4):
        deposit(s)
        weights(order[3 + s], s - 1)
    weights(order[7], 3)
    for load in loads[:2]:
        load.wait()

    def four_sources(j, _):
        k = 4 * j
        first, second = along_y((0, 1)), along_y((2, 3))
        deposit(0)
        deposit(1)
        weights(order[k + 4], 0)
        along_x(k - 4, first)
        deposit(2)
        weights(order[k + 5], 1)
        deposit(3)
        weights(order[k + 6], 2)
        along_x(k - 2, second)
        weights(order[k + 7], 3)
        return 0

    turns = (count + 1) // 4
    lax.fori_loop(1, turns, four_sources, 0)

    @pl.when(count > 4 * turns)
    def _():
        first, second = along_y((0, 1)), along_y((2, 3))
        for s in range(2):
            deposit(s)
        along_x(4 * turns - 4, first)
        third = along_y((0, 1))
        along_x(4 * turns - 2, second)
        along_x(4 * turns, third)

    @pl.when(count <= 4 * turns)
    def _():
        first, second = along_y((0, 1)), along_y((2, 3))
        along_x(4 * turns - 4, first)
        along_x(4 * turns - 2, second)

    for load in loads[2:]:
        load.wait()

    me = lax.axis_index("dom")
    index = lax.broadcasted_iota(jnp.int32, (ROWS, 128), 0).astype(F32)

    def multiply(target, _):
        def partner(j, add):
            c = pair_c[target * 8 + j]
            p = pair_p[target * 8 + j]
            for t in range(2 * ROWS // 32):
                rows = slice(32 * t, 32 * t + 32)
                re = spec[p, 0, rows]
                im = spec[p, 1, rows]
                sums = []
                for part in range(2):
                    kr = kv[c, part, 0, rows]
                    ki = kv[c, part, 1, rows]
                    real = kr * re - ki * im
                    imag = kr * im + ki * re
                    if add:
                        real = acc[target, part, 0, rows] + real
                        imag = acc[target, part, 1, rows] + imag
                    sums += [real, imag]
                for place, value in enumerate(sums):
                    acc[target, place // 2, place % 2, rows] = value

        def later(j, _):
            partner(j, True)
            return 0

        @pl.when(pair_count[target] == 0)
        def _():
            acc[target] = jnp.zeros_like(acc[target])

        @pl.when(pair_count[target] > 0)
        def _():
            partner(0, False)
            lax.fori_loop(1, pair_count[target], later, 0)

        return 0

    lax.fori_loop(0, 2 * BUN, multiply, 0)

    def finish(beam, _):
        firsts = []
        for b in range(BUN):
            target = beam * BUN + b
            stacks = []
            for part in range(2):
                rp, rm = acc[target, part, 0, :ROWS], acc[target, part, 0, ROWS:]
                ip, im = acc[target, part, 1, :ROWS], acc[target, part, 1, ROWS:]
                top = jnp.concatenate([rp + rm, ip + im], axis=1)
                low = jnp.concatenate([im - ip, rp - rm], axis=1)
                dh, dl = high_low(jnp.concatenate([top, low], axis=0))
                stacks.append(jnp.concatenate([dh, dl, dh], axis=0))
            firsts.append(mm(ix_ref[...], jnp.concatenate(stacks, axis=1)))
        for b, first in enumerate(firsts):
            for part in range(2):
                rows = slice((2 * b + part) * ROWS, (2 * b + part + 1) * ROWS)
                bh_ref[rows], bl_ref[rows] = high_low(first[:, 256 * part : 256 * part + 256])
        wide = mm(bh_ref[...], iy_ref[...])
        fields = wide[:, :128] + wide[:, 128:] + mm(bl_ref[...], iy_ref[:, :128])
        for b in range(BUN):
            for part in range(2):
                for i in range(SLICES):
                    top = (2 * b + part) * ROWS + 4 * i
                    win[beam, b, i, part] = fields[top : top + G, i : i + G]
            pltpu.make_async_copy(win.at[beam, b], f_any.at[beam, b], out_sem.at[beam]).start()
        products = []
        for b in range(BUN):
            y = jnp.broadcast_to(g_ref[doms + me, pl.ds(beam * 8 + 4 + b, 1), :], (ROWS, 128))
            yh, yl = high_low(jnp.maximum(0.0, 1.0 - jnp.abs(y - index)))
            fh, fl = high_low(fields[2 * b * ROWS : 2 * (b + 1) * ROWS, :ROWS])
            products.append(mm(jnp.concatenate([fh, fl], axis=0), jnp.concatenate([yh, yl], axis=1)))
        for b, both in enumerate(products):
            x = jnp.broadcast_to(g_ref[doms + me, pl.ds(beam * 8 + b, 1), :], (ROWS, 128))
            weight_x = jnp.maximum(0.0, 1.0 - jnp.abs(x - index))
            sampled = both[: 2 * ROWS, :128] + both[2 * ROWS :, :128] + both[: 2 * ROWS, 128:]
            for part in range(2):
                kick_ref[part, beam, b : b + 1, :] = jnp.sum(
                    weight_x * sampled[part * ROWS : (part + 1) * ROWS], axis=0, keepdims=True
                )
        return 0

    lax.fori_loop(0, 2, finish, 0)
    kicks = pltpu.make_async_copy(kick_ref, kick_any, enc_sem)
    kicks.start()
    for beam in range(2):
        pltpu.make_async_copy(win.at[beam], f_any.at[beam], out_sem.at[beam]).wait()
    kicks.wait()


def solve(gathered, enc):
    doms, particles = gathered.shape[0] // 3, gathered.shape[2]
    vmem = pl.BlockSpec(memory_space=pltpu.VMEM)
    anywhere = pl.BlockSpec(memory_space=pl.ANY)
    consts = [jnp.asarray(t) for t in tables(CHARGE / (particles * doms))]
    weight = pltpu.VMEM((2 * ROWS, doms * particles), BF)
    return pl.pallas_call(
        functools.partial(solve_kernel, doms),
        out_shape=(
            jax.ShapeDtypeStruct((2, BUN, SLICES, 2, G, G), F32),
            jax.ShapeDtypeStruct((2, 2, BUN, particles), F32),
        ),
        in_specs=[vmem] + [anywhere] * (1 + len(consts)),
        out_specs=(anywhere, anywhere),
        scratch_shapes=[pltpu.VMEM(t.shape, t.dtype) for t in consts] + [
            pltpu.SemaphoreType.DMA((len(consts),)),
            [weight] * 4,
            [weight] * 4,
            [pltpu.VMEM((ROWS, 3 * ROWS), BF)] * 4,
            pltpu.VMEM((2 * SRC + 4, 2, 2 * ROWS, 128), F32),
            pltpu.VMEM((2 * BUN, 2, 2, 2 * ROWS, 128), F32),
            pltpu.VMEM((BUN * 2 * ROWS, 256), BF),
            pltpu.VMEM((BUN * 2 * ROWS, 256), BF),
            pltpu.VMEM((2, BUN, SLICES, 2, G, G), F32),
            pltpu.VMEM((2, 2, BUN, particles), F32),
            pltpu.SMEM((3, 8, 128), jnp.int32),
            pltpu.SMEM((2 * SRC + 8,), jnp.int32),
            pltpu.SMEM((2 * SRC,), jnp.int32),
            pltpu.SMEM((2 * BUN * 8,), jnp.int32),
            pltpu.SMEM((2 * BUN * 8,), jnp.int32),
            pltpu.SMEM((2 * BUN,), jnp.int32),
            pltpu.SemaphoreType.DMA,
            pltpu.SemaphoreType.DMA((2,)),
        ],
        compiler_params=pltpu.CompilerParams(vmem_limit_bytes=24 * 1024 * 1024),
        name="solve",
    )(gathered, enc, *[pltpu.with_memory_space_constraint(t, pltpu.HBM) for t in consts])


def on_device(positions, slice_index, encounters):
    groups, doms = lax.axis_size("bunch"), lax.axis_size("dom")
    particles = positions.shape[3]
    anywhere = pl.BlockSpec(memory_space=pl.ANY)
    gathered, enc = pl.pallas_call(
        functools.partial(exchange_kernel, groups, doms),
        out_shape=(
            jax.ShapeDtypeStruct((3 * doms, 16, particles), F32),
            jax.ShapeDtypeStruct((3, 8, 128), jnp.int32),
        ),
        in_specs=[anywhere] * 3,
        out_specs=(anywhere, anywhere),
        scratch_shapes=[
            pltpu.VMEM(positions.shape, F32),
            pltpu.VMEM(slice_index.shape, jnp.int32),
            pltpu.VMEM(encounters.shape, jnp.int32),
            pltpu.VMEM((16, particles), F32),
            pltpu.VMEM((8, 128), jnp.int32),
            pltpu.SemaphoreType.DMA((3,)),
            pltpu.SemaphoreType.DMA((4,)),
        ],
        compiler_params=pltpu.CompilerParams(
            collective_id=0, has_side_effects=True, vmem_limit_bytes=1024 * 1024
        ),
        name="exchange",
    )(*[pltpu.with_memory_space_constraint(v, pltpu.HBM) for v in (positions, slice_index, encounters)])
    return solve(gathered, enc)


def solution(mesh):
    placed = (P(None, None, "bunch", "dom"), P(None, "bunch", "dom"), P("bunch", None))
    return jax.shard_map(
        on_device,
        mesh=mesh,
        in_specs=placed,
        out_specs=(P(None, "bunch", None, None, None, None), P(None, None, "bunch", "dom")),
        check_vma=False,
    )
```

```python
import functools

import jax
import jax.numpy as jnp
import ml_dtypes
import numpy as np
from jax import lax
from jax.experimental import pallas as pl
from jax.experimental.pallas import tpu as pltpu
from jax.sharding import PartitionSpec as P

G = 64
SLICES = 4
R = 3
NOFF = 7
CHARGE = 8.0
SOFTEN = 1.0

BUN = 4
SRC = BUN + 2 * R
ALWAYS = (SRC, 2 * SRC - 1, R - 1, R + BUN)
N1 = 152
N2 = 134
ROWS = 80
MESH = pl.DeviceIdType.MESH
BF = jnp.bfloat16
F32 = jnp.float32


def split_table(values):
    high = values.astype(ml_dtypes.bfloat16)
    low = (values - high.astype(np.float64)).astype(ml_dtypes.bfloat16)
    return high, low


@functools.lru_cache(maxsize=None)
def tables(scale):
    line = np.arange(ROWS)
    kx = np.arange(ROWS)
    live_kx = (kx <= N1 // 2).astype(np.float64)
    ky = np.arange(128)
    live_ky = (ky <= N2 // 2).astype(np.float64)

    phase_y = 2.0 * np.pi * (line[:, None] * ky[None, :] % N2) / N2
    along = np.concatenate([np.cos(phase_y) * live_ky, -np.sin(phase_y) * live_ky], axis=1)
    high, low = split_table(along)
    fwd_y = np.concatenate([high, high, low], axis=0)

    phase_x = 2.0 * np.pi * (kx[:, None] * line[None, :] % N1) / N1
    cos_x = np.cos(phase_x) * live_kx[:, None]
    sin_x = np.sin(phase_x) * live_kx[:, None]
    high, low = split_table(np.concatenate([cos_x, sin_x], axis=0))
    fwd_x = np.concatenate([high, high, low], axis=1)

    half = np.where((kx == 0) | (kx == N1 // 2), 0.5, 1.0) / (N1 * N2)
    high, low = split_table(np.concatenate([(cos_x * half[:, None]).T, (sin_x * half[:, None]).T], axis=1))
    inv_x = np.concatenate([high, high, low], axis=1)

    twice = np.where((ky == 0) | (ky == N2 // 2), 1.0, 2.0) * live_ky
    cell = np.arange(128)
    live_cell = (cell < G + SLICES - 1).astype(np.float64)
    phase = 2.0 * np.pi * (ky[:, None] * cell[None, :] % N2) / N2
    back = np.concatenate([np.cos(phase) * twice[:, None], -np.sin(phase) * twice[:, None]], axis=0)
    inv_y = np.concatenate(split_table(back * live_cell[None, :]), axis=1)

    d1 = np.arange(N1)
    d1 = np.where(d1 < N1 // 2, d1, d1 - N1).astype(np.float64)
    d2 = np.arange(N2)
    d2 = np.where(d2 < N2 // 2, d2, d2 - N2).astype(np.float64)
    spectra = np.zeros((NOFF, 2, 2, 2 * ROWS, 128), np.float32)
    rows = np.arange(N1 // 2 + 1)
    for column in range(NOFF):
        along_x = d1[:, None] + 20.0 * (column - R)
        along_y = d2[None, :] + 3.0 * (column - R)
        spread = along_x * along_x + along_y * along_y + SOFTEN
        for part, value in enumerate((along_x / spread, along_y / spread)):
            hat = np.fft.fft2(value)[:, : N2 // 2 + 1] * scale
            for half_index, pick in enumerate((rows, (-rows) % N1)):
                place = slice(half_index * ROWS, half_index * ROWS + rows.size)
                spectra[column, part, 0, place, : N2 // 2 + 1] = hat[pick].real
                spectra[column, part, 1, place, : N2 // 2 + 1] = hat[pick].imag
    return fwd_y, fwd_x, inv_x, inv_y, spectra


def exchange_kernel(
    groups, doms,
    pos_any, sl_any, enc_any, g_ref, e_ref,
    pos_ref, sl_ref, enc_ref, block, encs, in_sem, sems,
):
    n = lax.axis_index("bunch")
    me = lax.axis_index("dom")
    loads = [
        pltpu.make_async_copy(src, dst, in_sem.at[k])
        for k, (src, dst) in enumerate(((pos_any, pos_ref), (sl_any, sl_ref), (enc_any, enc_ref)))
    ]
    for load in loads:
        load.start()
    peers = []
    for off in (1, -1, 0):
        for j in range(doms):
            if off == 0 and j == 0:
                continue
            peers.append((off, lax.rem(n + off + groups, groups), lax.rem(me + j, doms)))

    barrier = pltpu.get_barrier_semaphore()
    for _, there, dom in peers:
        pl.semaphore_signal(barrier, inc=1, device_id=(there, dom), device_id_type=MESH)

    for load in loads:
        load.wait()
    centre = 0.5 * (G - 1)
    for beam in range(2):
        gap = sl_ref[beam].astype(F32)
        block[beam * 8 : beam * 8 + 4, :] = (centre + pos_ref[0, beam]) + 4.0 * gap
        block[beam * 8 + 4 : beam * 8 + 8, :] = (centre + pos_ref[1, beam]) + gap
    encs[...] = jnp.zeros_like(encs)
    encs[0:BUN, 0:NOFF] = enc_ref[...]
    pl.semaphore_wait(barrier, len(peers))

    for off in (1, -1):
        pltpu.make_async_remote_copy(
            src_ref=encs,
            dst_ref=e_ref.at[1 - off],
            send_sem=sems.at[0],
            recv_sem=sems.at[1],
            device_id=(lax.rem(n + off + groups, groups), me),
            device_id_type=MESH,
        ).start()
    for off, there, dom in peers:
        pltpu.make_async_remote_copy(
            src_ref=block,
            dst_ref=g_ref.at[(1 - off) * doms + me],
            send_sem=sems.at[2],
            recv_sem=sems.at[3],
            device_id=(there, dom),
            device_id_type=MESH,
        ).start()
    pltpu.make_async_copy(encs, e_ref.at[1], sems.at[1]).start()
    pltpu.make_async_copy(block, g_ref.at[doms + me], sems.at[3]).start()
    for sem, ref in ((3, g_ref), (1, e_ref), (2, g_ref.at[pl.ds(0, len(peers))]), (0, e_ref.at[pl.ds(0, 2)])):
        pltpu.make_async_copy(ref, ref, sems.at[sem]).wait()


def high_low(values):
    high = values.astype(BF)
    return high, (values - high.astype(F32)).astype(BF)


def mm(a, b):
    return jnp.dot(a, b, preferred_element_type=F32)


def live_lists(enc_ref, order, place, pair_t, pair_c, pair_p):
    flags = []
    for beam in range(2):
        for b in range(BUN):
            row = []
            for c in range(NOFF):
                if beam == 0:
                    row.append(enc_ref[1, b, c])
                else:
                    a = b + c + 1
                    row.append(enc_ref[a // BUN, a % BUN, 2 * R - c])
            flags.append(row)
    count = jnp.int32(0)
    for k in range(2 * SRC + 8):
        order[k] = 0
    for source in ALWAYS:
        place[source] = count
        order[count] = source
        count = count + 1
    for source in range(2 * SRC):
        if source in ALWAYS:
            continue
        beam, m = source // SRC, source % SRC
        users = [flags[(1 - beam) * BUN + b][m - b] for b in range(BUN) if 0 <= m - b < NOFF]
        need = users[0]
        for other in users[1:]:
            need = jnp.maximum(need, other)
        order[count] = source
        place[source] = count
        count = count + need
    order[count] = 0
    total = jnp.int32(0)
    for target in range(2 * BUN):
        beam, b = target // BUN, target % BUN
        for c in range(NOFF):
            pair_t[total] = target
            pair_c[total] = c
            pair_p[total] = place[(1 - beam) * SRC + b + c]
            total = total + flags[target][c]
    return count, total


def solve_kernel(
    doms,
    g_ref, enc_any, fy_any, fx_any, ix_any, iy_any, kv_any,
    f_any, kick_any,
    fy_ref, fx_ref, ix_ref, iy_ref, kv, table_sem,
    wx, wy, grids, spec, acc, bh_ref, bl_ref, win, kick_ref,
    enc_ref, order, place, pair_t, pair_c, pair_p, enc_sem, out_sem,
):
    enc_load = pltpu.make_async_copy(enc_any, enc_ref, enc_sem)
    enc_load.start()
    pairs = ((fy_any, fy_ref), (fx_any, fx_ref), (kv_any, kv), (ix_any, ix_ref), (iy_any, iy_ref))
    loads = [pltpu.make_async_copy(src, dst, table_sem.at[k]) for k, (src, dst) in enumerate(pairs)]
    for load in loads:
        load.start()

    line = lax.broadcasted_iota(jnp.int32, (16, 128), 0).astype(F32)
    lines = [(line + 16.0 * t).astype(BF) for t in range(ROWS // 16)]
    below = [(line + (16.0 * t - 1.0)).astype(BF) for t in range(ROWS // 16)]
    nothing = jnp.zeros((16, 128), BF)

    def weights(source, slot):
        beam = source // SRC
        m = source - beam * SRC
        grp = (m + 1) // BUN
        bunch = (m + 1) % BUN
        for coord, dest in ((0, wx[slot]), (1, wy[slot])):
            row = beam * 8 + coord * 4 + bunch
            for d in range(doms):
                at = jnp.broadcast_to(g_ref[grp * doms + d, pl.ds(row, 1), :], (8, 128))
                cell = jnp.floor(at)
                upper = at - cell
                lower = 1.0 - upper
                values = [cell, lower, lower - lower.astype(BF).astype(F32), upper, upper - upper.astype(BF).astype(F32)]
                cells, lh, ll, uh, ul = [jnp.concatenate([v, v], axis=0).astype(BF) for v in values]
                cols = slice(d * 128, (d + 1) * 128)
                for t in range(ROWS // 16):
                    first = lines[t] == cells
                    second = below[t] == cells
                    dest[16 * t : 16 * t + 16, cols] = jnp.where(first, lh, jnp.where(second, uh, nothing))
                    dest[ROWS + 16 * t : ROWS + 16 * t + 16, cols] = jnp.where(
                        first, ll, jnp.where(second, ul, nothing)
                    )

    def deposit(slot):
        both = lax.dot_general(
            wx[slot][...], wy[slot][...], (((1,), (1,)), ((), ())), preferred_element_type=F32
        )
        both = both[:ROWS] + both[ROWS:]
        high, low = high_low(both[:, :ROWS] + both[:, ROWS:])
        grids[slot][...] = jnp.concatenate([high, low, high], axis=1)

    def along_y(slots):
        return mm(jnp.concatenate([grids[slot][...] for slot in slots], axis=0), fy_ref[...])

    def along_x(k, first):
        outs = []
        for s in range(first.shape[0] // ROWS):
            high, low = high_low(first[s * ROWS : (s + 1) * ROWS])
            outs.append(mm(fx_ref[...], jnp.concatenate([high, low, high], axis=0)))
        for s, out in enumerate(outs):
            cr, ci = out[:ROWS, :128], out[:ROWS, 128:]
            sr, si = out[ROWS:, :128], out[ROWS:, 128:]
            spec[k + s, 0, :ROWS] = cr + si
            spec[k + s, 0, ROWS:] = cr - si
            spec[k + s, 1, :ROWS] = ci - sr
            spec[k + s, 1, ROWS:] = ci + sr

    for s in range(4):
        weights(ALWAYS[s], s)
    enc_load.wait()
    count, total = live_lists(enc_ref, order, place, pair_t, pair_c, pair_p)
    deposit(0)
    acc[...] = jnp.zeros_like(acc)
    for s in range(1, 4):
        deposit(s)
        weights(order[3 + s], s - 1)
    weights(order[7], 3)
    for load in loads[:2]:
        load.wait()

    def four_sources(j, _):
        k = 4 * j
        first, second = along_y((0, 1)), along_y((2, 3))
        deposit(0)
        deposit(1)
        weights(order[k + 4], 0)
        along_x(k - 4, first)
        deposit(2)
        weights(order[k + 5], 1)
        deposit(3)
        weights(order[k + 6], 2)
        along_x(k - 2, second)
        weights(order[k + 7], 3)
        return 0

    turns = (count + 1) // 4
    lax.fori_loop(1, turns, four_sources, 0)

    @pl.when(count > 4 * turns)
    def _():
        first, second = along_y((0, 1)), along_y((2, 3))
        for s in range(2):
            deposit(s)
        along_x(4 * turns - 4, first)
        third = along_y((0, 1))
        along_x(4 * turns - 2, second)
        along_x(4 * turns, third)

    @pl.when(count <= 4 * turns)
    def _():
        first, second = along_y((0, 1)), along_y((2, 3))
        along_x(4 * turns - 4, first)
        along_x(4 * turns - 2, second)

    for load in loads[2:]:
        load.wait()

    me = lax.axis_index("dom")
    index = lax.broadcasted_iota(jnp.int32, (ROWS, 128), 0).astype(F32)

    def multiply(j, _):
        target = pair_t[j]
        c = pair_c[j]
        p = pair_p[j]
        for t in range(2 * ROWS // 32):
            rows = slice(32 * t, 32 * t + 32)
            re = spec[p, 0, rows]
            im = spec[p, 1, rows]
            sums = []
            for part in range(2):
                kr = kv[c, part, 0, rows]
                ki = kv[c, part, 1, rows]
                sums.append(acc[target, part, 0, rows] + (kr * re - ki * im))
                sums.append(acc[target, part, 1, rows] + (kr * im + ki * re))
            for place_in, value in enumerate(sums):
                acc[target, place_in // 2, place_in % 2, rows] = value
        return 0

    lax.fori_loop(0, total, multiply, 0)

    def finish(beam, _):
        firsts = []
        for b in range(BUN):
            target = beam * BUN + b
            stacks = []
            for part in range(2):
                rp, rm = acc[target, part, 0, :ROWS], acc[target, part, 0, ROWS:]
                ip, im = acc[target, part, 1, :ROWS], acc[target, part, 1, ROWS:]
                top = jnp.concatenate([rp + rm, ip + im], axis=1)
                low = jnp.concatenate([im - ip, rp - rm], axis=1)
                dh, dl = high_low(jnp.concatenate([top, low], axis=0))
                stacks.append(jnp.concatenate([dh, dl, dh], axis=0))
            firsts.append(mm(ix_ref[...], jnp.concatenate(stacks, axis=1)))
        for b, first in enumerate(firsts):
            for part in range(2):
                rows = slice((2 * b + part) * ROWS, (2 * b + part + 1) * ROWS)
                bh_ref[rows], bl_ref[rows] = high_low(first[:, 256 * part : 256 * part + 256])
        wide = mm(bh_ref[...], iy_ref[...])
        fields = wide[:, :128] + wide[:, 128:] + mm(bl_ref[...], iy_ref[:, :128])
        for b in range(BUN):
            for part in range(2):
                for i in range(SLICES):
                    top = (2 * b + part) * ROWS + 4 * i
                    win[beam, b, i, part] = fields[top : top + G, i : i + G]
            pltpu.make_async_copy(win.at[beam, b], f_any.at[beam, b], out_sem.at[beam]).start()
        products = []
        for b in range(BUN):
            y = jnp.broadcast_to(g_ref[doms + me, pl.ds(beam * 8 + 4 + b, 1), :], (ROWS, 128))
            yh, yl = high_low(jnp.maximum(0.0, 1.0 - jnp.abs(y - index)))
            fh, fl = high_low(fields[2 * b * ROWS : 2 * (b + 1) * ROWS, :ROWS])
            products.append(mm(jnp.concatenate([fh, fl], axis=0), jnp.concatenate([yh, yl], axis=1)))
        for b, both in enumerate(products):
            x = jnp.broadcast_to(g_ref[doms + me, pl.ds(beam * 8 + b, 1), :], (ROWS, 128))
            weight_x = jnp.maximum(0.0, 1.0 - jnp.abs(x - index))
            sampled = both[: 2 * ROWS, :128] + both[2 * ROWS :, :128] + both[: 2 * ROWS, 128:]
            for part in range(2):
                kick_ref[part, beam, b : b + 1, :] = jnp.sum(
                    weight_x * sampled[part * ROWS : (part + 1) * ROWS], axis=0, keepdims=True
                )
        return 0

    lax.fori_loop(0, 2, finish, 0)
    kicks = pltpu.make_async_copy(kick_ref, kick_any, enc_sem)
    kicks.start()
    for beam in range(2):
        pltpu.make_async_copy(win.at[beam], f_any.at[beam], out_sem.at[beam]).wait()
    kicks.wait()


def solve(gathered, enc):
    doms, particles = gathered.shape[0] // 3, gathered.shape[2]
    vmem = pl.BlockSpec(memory_space=pltpu.VMEM)
    anywhere = pl.BlockSpec(memory_space=pl.ANY)
    consts = [jnp.asarray(t) for t in tables(CHARGE / (particles * doms))]
    weight = pltpu.VMEM((2 * ROWS, doms * particles), BF)
    return pl.pallas_call(
        functools.partial(solve_kernel, doms),
        out_shape=(
            jax.ShapeDtypeStruct((2, BUN, SLICES, 2, G, G), F32),
            jax.ShapeDtypeStruct((2, 2, BUN, particles), F32),
        ),
        in_specs=[vmem] + [anywhere] * (1 + len(consts)),
        out_specs=(anywhere, anywhere),
        scratch_shapes=[pltpu.VMEM(t.shape, t.dtype) for t in consts] + [
            pltpu.SemaphoreType.DMA((len(consts),)),
            [weight] * 4,
            [weight] * 4,
            [pltpu.VMEM((ROWS, 3 * ROWS), BF)] * 4,
            pltpu.VMEM((2 * SRC + 4, 2, 2 * ROWS, 128), F32),
            pltpu.VMEM((2 * BUN, 2, 2, 2 * ROWS, 128), F32),
            pltpu.VMEM((BUN * 2 * ROWS, 256), BF),
            pltpu.VMEM((BUN * 2 * ROWS, 256), BF),
            pltpu.VMEM((2, BUN, SLICES, 2, G, G), F32),
            pltpu.VMEM((2, 2, BUN, particles), F32),
            pltpu.SMEM((3, 8, 128), jnp.int32),
            pltpu.SMEM((2 * SRC + 8,), jnp.int32),
            pltpu.SMEM((2 * SRC,), jnp.int32),
            pltpu.SMEM((2 * BUN * 8,), jnp.int32),
            pltpu.SMEM((2 * BUN * 8,), jnp.int32),
            pltpu.SMEM((2 * BUN * 8,), jnp.int32),
            pltpu.SemaphoreType.DMA,
            pltpu.SemaphoreType.DMA((2,)),
        ],
        compiler_params=pltpu.CompilerParams(vmem_limit_bytes=24 * 1024 * 1024),
        name="solve",
    )(gathered, enc, *[pltpu.with_memory_space_constraint(t, pltpu.HBM) for t in consts])


def on_device(positions, slice_index, encounters):
    groups, doms = lax.axis_size("bunch"), lax.axis_size("dom")
    particles = positions.shape[3]
    anywhere = pl.BlockSpec(memory_space=pl.ANY)
    gathered, enc = pl.pallas_call(
        functools.partial(exchange_kernel, groups, doms),
        out_shape=(
            jax.ShapeDtypeStruct((3 * doms, 16, particles), F32),
            jax.ShapeDtypeStruct((3, 8, 128), jnp.int32),
        ),
        in_specs=[anywhere] * 3,
        out_specs=(anywhere, anywhere),
        scratch_shapes=[
            pltpu.VMEM(positions.shape, F32),
            pltpu.VMEM(slice_index.shape, jnp.int32),
            pltpu.VMEM(encounters.shape, jnp.int32),
            pltpu.VMEM((16, particles), F32),
            pltpu.VMEM((8, 128), jnp.int32),
            pltpu.SemaphoreType.DMA((3,)),
            pltpu.SemaphoreType.DMA((4,)),
        ],
        compiler_params=pltpu.CompilerParams(
            collective_id=0, has_side_effects=True, vmem_limit_bytes=1024 * 1024
        ),
        name="exchange",
    )(*[pltpu.with_memory_space_constraint(v, pltpu.HBM) for v in (positions, slice_index, encounters)])
    return solve(gathered, enc)


def solution(mesh):
    placed = (P(None, None, "bunch", "dom"), P(None, "bunch", "dom"), P("bunch", None))
    return jax.shard_map(
        on_device,
        mesh=mesh,
        in_specs=placed,
        out_specs=(P(None, "bunch", None, None, None, None), P(None, None, "bunch", "dom")),
        check_vma=False,
    )
```
